32 devices in a mesh: sec: 4 (over y, x), vel: 8 (over z, core).
Axes of the slice: x: 2, y: 2, z: 4, core: 2. Of those that a mesh axis runs over, the one named last changes fastest.
Arguments:
- distribution: float32 [13824, 1024], P('vel', 'sec'), may hold values from -6 to 6
- collision: float32 [1024], P('sec'), may hold values from 0.05 to 2
- lower_blocks: float32 [25, 1024], P(None, 'sec'), may hold values from -0.6 to 0.6
- upper_blocks: float32 [25, 1024], P(None, 'sec'), may hold values from -0.6 to 0.6
- diag_inverse: float32 [25, 1024], P(None, 'sec'), may hold values from -0.2 to 1.4
Outputs:
- new_distribution: float32 [13824, 1024], P('vel', 'sec')
- macro: float32 [5, 1024], P(None, 'sec')
The draws below stay inside these ranges and needn't reach their ends.
All inputs are finite; a program needn't handle non-finite values.
Results may differ from the reference program's by a relative error of at most 0.0003.
Values sent between devices are 32-bit elements; how exact they have to be, the bound alone decides.
A program may use at most 64 MiB of HBM per device.

```python
import math
import jax
import jax.numpy as jnp
import numpy as np
from jax import lax

NXI = 24
NV = 13824
TUBES = 128
JACOBI = 4
NEWTON = 2
NL = 8
NC = 1024


def draw_diag_inverse(key, part):
    diag_key, off_key = jax.random.split(jax.random.fold_in(key, 7))
    diagonal = jax.random.uniform(diag_key, (5, 1, NC), jnp.float32, 0.7, 1.3)
    offdiag = jnp.clip(0.08 * jax.random.normal(off_key, (5, 5, NC), jnp.float32), -0.2, 0.2)
    identity = jnp.eye(5, dtype=jnp.float32)[:, :, None]
    matrices = identity * diagonal + (1.0 - identity) * offdiag
    return matrices.reshape(25, NC)


def shard_levels(stream_key, extent, cuts, low, largest):
    def one(position, shards_of):
        draws = jax.random.uniform(jax.random.fold_in(jax.random.fold_in(stream_key, 6), position), (shards_of,), jnp.float32, low / len(cuts), largest / len(cuts))
        return jnp.repeat(jnp.exp(draws), extent[position] // shards_of).reshape((-1,) + (1,) * (len(extent) - position - 1))

    factor_of = one(*cuts[0])
    for cut in cuts[1:]:
        factor_of = factor_of * one(*cut)
    return factor_of


def scatter_about(rng, dims, deviation, bound, shards=(), held_as=jnp.bfloat16):
    drawn = deviation * jax.random.normal(rng, dims, jnp.float32)
    if shards:
        drawn = drawn * shard_levels(rng, dims, shards, -0.22, 0.18)
    return jnp.clip(drawn, -bound, bound).astype(held_as)


def setup_inputs(seed: int = 0) -> dict:
    keys = jax.random.split(jax.random.key(seed), 6)
    return {
        "distribution": scatter_about(keys[0], (NV, NC), 1.0, 6.0, ((0, 8), (1, 4)), jnp.float32),
        "collision": jnp.clip(jnp.exp(math.log(2.0) - 3.6888794 * jax.random.uniform(keys[1], (NC,), jnp.float32) ** shard_levels(keys[1], (NC,), ((0, 4),), -0.2, 0.2)), 0.05, 2.0),
        "lower_blocks": scatter_about(keys[2], (25, NC), 0.15, 0.6, ((1, 4),), jnp.float32),
        "upper_blocks": scatter_about(keys[3], (25, NC), 0.15, 0.6, ((1, 4),), jnp.float32),
        "diag_inverse": draw_diag_inverse(jax.random.fold_in(keys[5], 71), 0),
    }


HIGH = lax.Precision.HIGHEST
pseudo_rate = 1.0

def hermite_rule(count):
    quarter = math.pi ** (-0.25)
    found = []
    last_slope = 1.0
    for index in range(count // 2):
        if index == 0:
            guess = math.sqrt(2.0 * count + 1.0) - 1.85575 * (2.0 * count + 1.0) ** (-0.16667)
        elif index == 1:
            guess = guess - 1.14 * count ** 0.426 / guess
        elif index == 2:
            guess = 1.86 * guess - 0.86 * found[0][0]
        elif index == 3:
            guess = 1.91 * guess - 0.91 * found[1][0]
        else:
            guess = 2.0 * guess - found[index - 2][0]
        for repeat in range(60):
            current = quarter
            previous = 0.0
            for order in range(count):
                older = previous
                previous = current
                current = guess * math.sqrt(2.0 / (order + 1)) * previous - math.sqrt(order / (order + 1.0)) * older
            last_slope = math.sqrt(2.0 * count) * previous
            guess = guess - current / last_slope
        found.append((guess, 2.0 / (last_slope * last_slope)))
    positive = found[::-1]
    points = [-pair[0] for pair in found] + [pair[0] for pair in positive]
    weights = [pair[1] for pair in found] + [pair[1] for pair in positive]
    return (np.array(points), np.array(weights))

def node_tables(axis_points):
    points, weights = hermite_rule(axis_points)
    node_index = np.arange(axis_points ** 3)
    idx_x = node_index % axis_points
    idx_z = node_index // axis_points % axis_points
    idx_y = node_index // (axis_points * axis_points)
    along_x = points[idx_x]
    along_y = points[idx_y]
    along_z = points[idx_z]
    node_weight = weights[idx_x] * weights[idx_y] * weights[idx_z] / math.pi ** 1.5
    energy = along_x ** 2 + along_y ** 2 + along_z ** 2 - 1.5
    moment_basis = np.stack([along_x * 0.0 + 1.0, along_x, along_y, along_z, energy])
    norm_scale = np.array([1.0, 0.5, 0.5, 0.5, 1.5])
    return (along_x, node_weight, moment_basis * node_weight[None, :], moment_basis / norm_scale[:, None])

def apply_block(matrices, vector):
    shaped = matrices.reshape((5, 5) + vector.shape[1:])
    return lax.optimization_barrier(jnp.sum(shaped * vector[None], axis=1))

def newton_sums(loaded, signed, shift_mass, shift_flow):
    growth = jnp.exp(shift_mass + shift_flow * signed)
    scaled = loaded * growth
    excess = loaded * (growth - 1.0)
    return jnp.stack([jnp.sum(scaled), jnp.sum(scaled * signed), jnp.sum(scaled * signed * signed), jnp.sum(excess), jnp.sum(excess * signed)])

def newton_update(shift_mass, shift_flow, sums, goal_mass, goal_flow):
    resid_mass = sums[3] - goal_mass
    resid_flow = sums[4] - goal_flow
    determinant = sums[0] * sums[2] - sums[1] * sums[1]
    new_mass = shift_mass - (sums[2] * resid_mass - sums[1] * resid_flow) / determinant
    new_flow = shift_flow - (sums[0] * resid_flow - sums[1] * resid_mass) / determinant
    return (new_mass, new_flow)

def reference(distribution, collision, lower_blocks, upper_blocks, diag_inverse):
    along_x, node_weight, weighted_np, rebuild_np = node_tables(NXI)
    weighted = jnp.asarray(weighted_np, jnp.float32)
    rebuild = jnp.asarray(rebuild_np, jnp.float32)
    signed = jnp.asarray(along_x, jnp.float32)
    node_mass = jnp.asarray(node_weight, jnp.float32)
    old_moments = jnp.dot(weighted, distribution, precision=HIGH)
    target = jnp.dot(rebuild.T, old_moments, precision=HIGH)
    thickness = collision.reshape(NL, TUBES)

    def sweep_block(inputs):
        goal_part, heading, old_part = inputs
        node_speed = jnp.abs(heading)[:, None, None]
        denominator = node_speed * NL + thickness[None] + pseudo_rate
        carry_rate = node_speed * NL / denominator
        drive_term = (thickness[None] * goal_part + pseudo_rate * old_part) / denominator

        def advance(carried, inputs_here):
            value = inputs_here[0] * carried + inputs_here[1]
            return (value, value)
        start = jnp.zeros((goal_part.shape[0], TUBES), jnp.float32)
        rate_lines = jnp.moveaxis(carry_rate, 1, 0)
        drive_lines = jnp.moveaxis(drive_term, 1, 0)
        _, forward = lax.scan(advance, start, (rate_lines, drive_lines))
        _, backward = lax.scan(advance, start, (rate_lines, drive_lines), reverse=True)
        chosen = jnp.where(heading[None, :, None] > 0, forward, backward)
        return jnp.moveaxis(chosen, 0, 1)
    plane = NXI * NXI
    swept = lax.map(sweep_block, (target.reshape(NXI, plane, NL, TUBES), signed.reshape(NXI, plane), distribution.reshape(NXI, plane, NL, TUBES)))
    half_field = swept.reshape(NV, NC)
    half_moments = jnp.dot(weighted, half_field, precision=HIGH)
    residual = (half_moments - old_moments).reshape(5, NL, TUBES)
    lower_r = lower_blocks.reshape(25, NL, TUBES)
    upper_r = upper_blocks.reshape(25, NL, TUBES)
    inverse_r = diag_inverse.reshape(25, NL, TUBES)
    correction = apply_block(inverse_r, residual)
    edge_zero = jnp.zeros((5, 1, TUBES), jnp.float32)
    for sweep_index in range(JACOBI):
        from_left = jnp.concatenate([edge_zero, correction[:, :-1]], axis=1)
        from_right = jnp.concatenate([correction[:, 1:], edge_zero], axis=1)
        correction = apply_block(inverse_r, residual - apply_block(lower_r, from_left) - apply_block(upper_r, from_right))
    correction = correction.reshape(5, NC)
    macro = half_moments + correction
    synthetic = half_field + jnp.dot(rebuild.T, correction, precision=HIGH)
    totals = lax.optimization_barrier(jnp.sum(old_moments - macro, axis=1))
    loaded = node_mass * lax.optimization_barrier(jnp.sum(jnp.abs(synthetic), axis=1))
    shift_mass = jnp.zeros((), jnp.float32)
    shift_flow = jnp.zeros((), jnp.float32)
    for newton_turn in range(NEWTON):
        sums = newton_sums(loaded, signed, shift_mass, shift_flow)
        shift_mass, shift_flow = newton_update(shift_mass, shift_flow, sums, totals[0], totals[1])
    growth = jnp.exp(shift_mass + shift_flow * signed)
    new_distribution = synthetic + jnp.abs(synthetic) * (growth[:, None] - 1.0)
    return (new_distribution, macro)
```

```python
import functools
import math

import jax
import jax.numpy as jnp
import numpy as np
from jax import lax
from jax.experimental import pallas as pl
from jax.experimental.pallas import tpu as pltpu
from jax.sharding import PartitionSpec as P

NXI = 24
TUBES = 128
JACOBI = 4
NEWTON = 2
CHUNKS = 6
PROWS = 80
pseudo_rate = 1.0
MESH = pl.DeviceIdType.MESH


def hermite_rule(count):
    quarter = math.pi ** (-0.25)
    found = []
    last_slope = 1.0
    for index in range(count // 2):
        if index == 0:
            guess = math.sqrt(2.0 * count + 1.0) - 1.85575 * (2.0 * count + 1.0) ** (-0.16667)
        elif index == 1:
            guess = guess - 1.14 * count**0.426 / guess
        elif index == 2:
            guess = 1.86 * guess - 0.86 * found[0][0]
        elif index == 3:
            guess = 1.91 * guess - 0.91 * found[1][0]
        else:
            guess = 2.0 * guess - found[index - 2][0]
        for repeat in range(60):
            current = quarter
            previous = 0.0
            for order in range(count):
                older = previous
                previous = current
                current = (
                    guess * math.sqrt(2.0 / (order + 1)) * previous
                    - math.sqrt(order / (order + 1.0)) * older
                )
            last_slope = math.sqrt(2.0 * count) * previous
            guess = guess - current / last_slope
        found.append((guess, 2.0 / (last_slope * last_slope)))
    positive = found[::-1]
    points = [-pair[0] for pair in found] + [pair[0] for pair in positive]
    weights = [pair[1] for pair in found] + [pair[1] for pair in positive]
    return (np.array(points), np.array(weights))


def tables():
    points, weights = hermite_rule(NXI)
    h = weights / math.sqrt(math.pi)
    y = np.repeat(points, NXI)
    z = np.tile(points, NXI)
    g = np.repeat(h, NXI) * np.tile(h, NXI)
    e = y * y + z * z - 1.0
    rows = np.concatenate([g, g * y, g * z, g * e, y, z, e]).astype(np.float32)
    cols = np.zeros((40, 128))
    x = points
    listed = [np.abs(x), 2.0 * x, (x * x - 0.5) / 1.5, h, h * x, h * (x * x - 0.5), x]
    for k, column in enumerate(listed):
        cols[:24, k] = column
    for lane in range(3):
        cols[24:32, lane] = x[lane * 8 : lane * 8 + 8]
        cols[32:40, lane] = h[lane * 8 : lane * 8 + 8]
    return rows, cols.astype(np.float32)


def kernel(
    n_sec, n_vel, length, rows,
    table, cols, dist, coll, lower, upper, diag,
    syn_out, grow_out, macro_out,
    dv, syn, out_p, out_n, in_p, in_n, s_part, s_recv, s_all, pb,
    om, hm, co, mac, t_all, w_tab, t_loc, ld_own, ld_sec, ld_rv, ld_rs,
    dist_sem, syn_sem, p_send, p_recv, n_send, n_recv,
    a1_send, a1_recv, a2_send, a2_recv, a3_send, a3_recv,
    pb_send, pb_recv, b1_send, b1_recv, b2_send, b2_recv,
):
    s = lax.axis_index("sec")
    v = lax.axis_index("vel")
    total = n_sec * length
    slices = 4 * length
    pairs = rows // 2
    per = pairs // CHUNKS
    all_rows = NXI * NXI

    load = pltpu.make_async_copy(dist, dv, dist_sem)
    load.start()
    barrier = pltpu.get_barrier_semaphore()
    for d in range(1, n_vel):
        pl.semaphore_signal(
            barrier, inc=1, device_id={"vel": lax.rem(v + d, n_vel)}, device_id_type=MESH
        )
    for d in range(1, n_sec):
        pl.semaphore_signal(
            barrier, inc=1, device_id={"sec": lax.rem(s + d, n_sec)}, device_id_type=MESH
        )

    def remote(src, dst, send, recv, where):
        return pltpu.make_async_remote_copy(
            src_ref=src, dst_ref=dst, send_sem=send, recv_sem=recv,
            device_id=where, device_id_type=MESH,
        )

    def column(k):
        return jnp.broadcast_to(cols[0:24, k : k + 1], (24, TUBES))

    sub = lax.broadcasted_iota(jnp.int32, (8, TUBES), 0)
    low = sub < 4
    pos = lax.broadcasted_iota(jnp.int32, (24, TUBES), 0) >= 12
    reach = column(0) * float(total)

    for p in range(length):
        lanes = slice(p * TUBES, (p + 1) * TUBES)
        base = (s * length + p) * PROWS
        for k, block in enumerate((lower, upper, diag)):
            for e in range(25):
                pb[pl.ds(base + k * 25 + e, 1), :] = block[e : e + 1, lanes]
        pb[pl.ds(base + 75, 1), :] = coll[0:1, lanes]
    inv, rate = [], []
    for p in range(length):
        den = reach + coll[0:1, p * TUBES : (p + 1) * TUBES] + pseudo_rate
        i = 1.0 / den
        inv.append(i)
        rate.append(reach * i)
    zero = jnp.zeros((24, TUBES), jnp.float32)
    w = [[zero] * length for _ in range(length)]
    a = [zero] * length
    fw = None
    for p in range(length):
        row = [rate[p] * e for e in fw[0]] + [inv[p]] if fw else [inv[p]]
        carry = rate[p] * fw[1] if fw else rate[p]
        fw = (row, carry)
        for q in range(p + 1):
            w[p][q] = jnp.where(pos, row[q], w[p][q])
        a[p] = jnp.where(pos, carry, a[p])
    bw = None
    for p in reversed(range(length)):
        row = [inv[p]] + [rate[p] * e for e in bw[0]] if bw else [inv[p]]
        carry = rate[p] * bw[1] if bw else rate[p]
        bw = (row, carry)
        for k in range(len(row)):
            w[p][p + k] = jnp.where(pos, w[p][p + k], row[k])
        a[p] = jnp.where(pos, a[p], carry)
    for p in range(length):
        for q in range(length):
            w_tab[p * (length + 1) + q] = w[p][q]
        w_tab[p * (length + 1) + length] = a[p]
    last = [jnp.where(pos, w[length - 1][q], w[0][q]) for q in range(length)]
    through = jnp.where(pos, a[length - 1], a[0])
    mix = through[8:16]
    mix_r = pltpu.roll(mix, 4, 0)
    thr_n = jnp.concatenate([through[0:8], through[0:8], jnp.where(low, mix, mix_r)], axis=0)
    thr_p = jnp.concatenate([through[16:24], through[16:24], jnp.where(low, mix_r, mix)], axis=0)

    @pl.when(s == 0)
    def _():
        in_p[...] = jnp.zeros_like(in_p)

    @pl.when(s == n_sec - 1)
    def _():
        in_n[...] = jnp.zeros_like(in_n)

    pl.semaphore_wait(barrier, n_vel + n_sec - 2)
    load.wait()

    def chunk(c):
        return pl.ds(c * per, per)

    def pos_copy(c):
        to = jnp.minimum(s + 1, n_sec - 1)
        return remote(out_p.at[chunk(c)], in_p.at[chunk(c)], p_send.at[c], p_recv.at[c], {"sec": to})

    def neg_copy(c):
        to = jnp.maximum(s - 1, 0)
        return remote(out_n.at[chunk(c)], in_n.at[chunk(c)], n_send.at[c], n_recv.at[c], {"sec": to})

    def first_pass(k, acc):
        acc = list(acc)
        bs = []
        for half in range(2):
            r = 2 * k + half
            at = v * rows + r
            d = [
                dv[pl.ds(pl.multiple_of(k * 48, 8) + half * 24, 24), p * TUBES : (p + 1) * TUBES]
                for p in range(length)
            ]
            for q in range(4):
                scale = table[q * all_rows + at]
                for p in range(length):
                    acc[p * 4 + q] = acc[p * 4 + q] + scale * d[p]
            b = last[0] * d[0]
            for p in range(1, length):
                b = b + last[p] * d[p]
            bs.append(b)
        b0, b1 = bs
        out_n[k, 0:8] = b0[0:8]
        out_n[k, 8:16] = b1[0:8]
        out_n[k, 16:24] = jnp.where(low, b0[8:16], pltpu.roll(b1[8:16], 4, 0))
        out_p[k, 0:8] = b0[16:24]
        out_p[k, 8:16] = b1[16:24]
        out_p[k, 16:24] = jnp.where(low, pltpu.roll(b0[8:16], 4, 0), b1[8:16])
        return tuple(acc)

    acc = (zero,) * slices
    for c in range(CHUNKS):
        acc = lax.fori_loop(c * per, (c + 1) * per, first_pass, acc)

        @pl.when(s == 0)
        def _():
            pos_copy(c).start()

        @pl.when(s == n_sec - 1)
        def _():
            neg_copy(c).start()

    for k in range(slices):
        s_part[k] = acc[k]

    def when_owner(index, run):
        if n_vel == slices:
            run()
        else:
            pl.when(index < slices)(run)

    def a1(d):
        to = lax.rem(v + d, n_vel)
        slot = jnp.minimum(to, slices - 1)
        return remote(s_part.at[slot], s_recv.at[d - 1], a1_send.at[d - 1], a1_recv.at[d - 1], {"vel": to})

    for d in range(1, n_vel):
        when_owner(lax.rem(v + d, n_vel), lambda: a1(d).start())

    own = pl.ds(s * length * PROWS, length * PROWS)

    def pb_copy(d):
        to = lax.rem(s + d, n_sec)
        return remote(pb.at[own], pb.at[own], pb_send.at[d - 1], pb_recv.at[d - 1], {"sec": to})

    def pb_wait(d):
        frm = lax.rem(s + n_sec - d, n_sec)
        there = pl.ds(frm * length * PROWS, length * PROWS)
        remote(pb.at[there], pb.at[there], pb_send.at[d - 1], pb_recv.at[d - 1], {"sec": frm}).wait_recv()

    for d in range(1, n_sec):
        pb_copy(d).start()

    mine = jnp.minimum(v, slices - 1)

    def a2(d, slot, to):
        return remote(
            s_all.at[mine, slot], s_all.at[mine, slot], a2_send.at[d - 1], a2_recv.at[d - 1], {"sec": to}
        )

    def reduce_slices():
        got = s_part[mine]
        for d in range(1, n_vel):
            a1(d).wait_recv()
            got = got + s_recv[d - 1]
        s_all[mine, s] = got
        for d in range(1, n_sec):
            a2(d, s, lax.rem(s + d, n_sec)).start()

    when_owner(v, reduce_slices)

    def relay(c):
        def forward_pos():
            pos_copy(c).wait_recv()

            @pl.when(s < n_sec - 1)
            def _():
                out_p[chunk(c)] = out_p[chunk(c)] + thr_p[None] * in_p[chunk(c)]
                pos_copy(c).start()

        def forward_neg():
            neg_copy(c).wait_recv()

            @pl.when(s > 0)
            def _():
                out_n[chunk(c)] = out_n[chunk(c)] + thr_n[None] * in_n[chunk(c)]
                neg_copy(c).start()

        @pl.when(s < n_sec // 2)
        def _():
            pl.when(s > 0)(forward_pos)
            forward_neg()

        @pl.when(s >= n_sec // 2)
        def _():
            pl.when(s < n_sec - 1)(forward_neg)
            forward_pos()

    def a3(d, slot, to):
        return remote(s_all.at[slot], s_all.at[slot], a3_send.at[d - 1], a3_recv.at[d - 1], {"vel": to})

    def gather_slices():
        for d in range(1, n_sec):
            frm = lax.rem(s + n_sec - d, n_sec)
            a2(d, frm, frm).wait_recv()
        for d in range(1, n_vel):
            a3(d, mine, lax.rem(v + d, n_vel)).start()

    relay(0)
    when_owner(v, gather_slices)
    for c in range(1, CHUNKS):
        relay(c)
    for d in range(1, n_vel):
        frm = lax.rem(v + n_vel - d, n_vel)
        when_owner(frm, lambda: a3(d, jnp.minimum(frm, slices - 1), frm).wait_recv())
    for d in range(1, n_sec):
        pb_wait(d)

    hx, hxx, hxe = column(3), column(4), column(5)
    x2, en = column(1), column(2)

    def total_of(value):
        return jnp.sum(value, axis=0, keepdims=True)

    for at in range(total):
        sec, p = at // length, at % length
        s0, s2, s3, s4 = [s_all[p * 4 + q, sec] for q in range(4)]
        om[0 * total + at : 0 * total + at + 1] = total_of(hx * s0)
        om[1 * total + at : 1 * total + at + 1] = total_of(hxx * s0)
        om[2 * total + at : 2 * total + at + 1] = total_of(hx * s2)
        om[3 * total + at : 3 * total + at + 1] = total_of(hx * s3)
        om[4 * total + at : 4 * total + at + 1] = total_of(hxe * s0 + hx * s4)

    thick, invs, rates = [], [], []
    for at in range(total):
        t = pb[at * PROWS + 75 : at * PROWS + 76]
        i = 1.0 / (reach + t + pseudo_rate)
        thick.append(t)
        invs.append(i)
        rates.append(reach * i)
    turned = [jnp.where(pos, rates[i], rates[total - 1 - i]) for i in range(total)]

    def sweep(drive):
        found, carried = [], None
        for i in range(total):
            here = jnp.where(pos, drive[i], drive[total - 1 - i])
            carried = here if carried is None else turned[i] * carried + here
            found.append(carried)
        return [jnp.where(pos, found[i], found[total - 1 - i]) for i in range(total)]

    halves = {}
    for q, norm in enumerate((1.0, 0.5, 0.5, 1.0)):
        goals, parts = [], []
        for at in range(total):
            m = [om[j * total + at : j * total + at + 1] for j in range(5)]
            if q == 0:
                goal = thick[at] * (m[0] + x2 * m[1] + en * m[4])
            elif q == 3:
                goal = jnp.broadcast_to(thick[at] * m[4] * (1.0 / 1.5), (24, TUBES))
            else:
                goal = jnp.broadcast_to(thick[at] * m[q + 1] * 2.0, (24, TUBES))
            sec, p = at // length, at % length
            goals.append(goal * invs[at])
            parts.append((s_all[p * 4 + q, sec] + norm * goal) * invs[at])
        swept = sweep(goals)
        for at in range(total):
            t_all[q * total + at] = swept[at]
        swept = sweep(parts)
        for at in range(total):
            f = swept[at]
            if q == 0:
                hm[at : at + 1] = total_of(hx * f)
                hm[total + at : total + at + 1] = total_of(hxx * f)
                halves[at] = hxe * f
            elif q == 3:
                hm[4 * total + at : 4 * total + at + 1] = total_of(halves[at] + hx * f)
            else:
                j = q + 1
                hm[j * total + at : j * total + at + 1] = total_of(hx * f)

    place = lax.broadcasted_iota(jnp.int32, (total, TUBES), 0)
    old = [om[j * total : (j + 1) * total] for j in range(5)]
    half = [hm[j * total : (j + 1) * total] for j in range(5)]
    resid = [half[j] - old[j] for j in range(5)]

    def entry(e):
        return pb[pl.ds(e, total, stride=PROWS), :]

    def apply_block(first, vector):
        out = []
        for i in range(5):
            value = entry(first + i * 5) * vector[0]
            for j in range(1, 5):
                value = value + entry(first + i * 5 + j) * vector[j]
            out.append(value)
        return out

    corr = apply_block(50, resid)
    for _ in range(JACOBI):
        left = [jnp.where(place == 0, 0.0, pltpu.roll(c, 1, 0)) for c in corr]
        right = [jnp.where(place == total - 1, 0.0, pltpu.roll(c, total - 1, 0)) for c in corr]
        lo = apply_block(0, left)
        up = apply_block(25, right)
        corr = apply_block(50, [resid[j] - lo[j] - up[j] for j in range(5)])
    goal = []
    for j in range(5):
        macro = half[j] + corr[j]
        co[j * total : (j + 1) * total] = corr[j]
        mac[j * total : (j + 1) * total] = macro
        if j < 2:
            change = jnp.sum(old[j] - macro, axis=0, keepdims=True)
            goal.append(jnp.sum(change, axis=1, keepdims=True))
    for p in range(length):
        at = s * length + p
        c = [co[pl.ds(j * total + at, 1), :] for j in range(5)]
        for j in range(5):
            macro_out[j : j + 1, p * TUBES : (p + 1) * TUBES] = mac[pl.ds(j * total + at, 1), :]
        t_loc[p * 4 + 0] = t_all[0 * total + at] + (c[0] + x2 * c[1] + en * c[4])
        t_loc[p * 4 + 1] = t_all[1 * total + at] + 2.0 * c[2]
        t_loc[p * 4 + 2] = t_all[2 * total + at] + 2.0 * c[3]
        t_loc[p * 4 + 3] = t_all[3 * total + at] + c[4] * (1.0 / 1.5)

    def second_pass(k, acc):
        n_mix, p_mix = in_n[k, 16:24], in_p[k, 16:24]
        flow = (
            jnp.concatenate(
                [in_n[k, 0:8], jnp.where(low, n_mix, pltpu.roll(p_mix, 4, 0)), in_p[k, 0:8]], axis=0
            ),
            jnp.concatenate(
                [in_n[k, 8:16], jnp.where(low, pltpu.roll(n_mix, 4, 0), p_mix), in_p[k, 8:16]], axis=0
            ),
        )
        for half_row in range(2):
            at = v * rows + 2 * k + half_row
            here = pl.ds(pl.multiple_of(k * 48, 8) + half_row * 24, 24)
            g = table[at]
            y = table[4 * all_rows + at]
            z = table[5 * all_rows + at]
            e = table[6 * all_rows + at]
            d = [dv[here, p * TUBES : (p + 1) * TUBES] for p in range(length)]
            size = None
            for p in range(length):
                f = t_loc[p * 4] + y * t_loc[p * 4 + 1] + z * t_loc[p * 4 + 2] + e * t_loc[p * 4 + 3]
                f = f + w_tab[p * (length + 1) + length] * flow[half_row]
                for q in range(length):
                    f = f + w_tab[p * (length + 1) + q] * d[q]
                syn[here, p * TUBES : (p + 1) * TUBES] = f
                size = jnp.abs(f) if size is None else size + jnp.abs(f)
            acc = acc + g * size
        return acc

    acc = zero
    stores = []
    for c in range(CHUNKS):
        acc = lax.fori_loop(c * per, (c + 1) * per, second_pass, acc)
        part = pl.ds(c * per * 48, per * 48)
        store = pltpu.make_async_copy(syn.at[part], syn_out.at[part], syn_sem.at[c])
        store.start()
        stores.append(store)

    lane = lax.broadcasted_iota(jnp.int32, (8, TUBES), 1)
    one = jnp.sum(acc, axis=1, keepdims=True)
    packed = jnp.where(lane == 0, one[0:8], jnp.where(lane == 1, one[8:16], one[16:24]))
    ld_own[...] = packed
    b1 = [
        remote(ld_own, ld_rv.at[d - 1], b1_send.at[d - 1], b1_recv.at[d - 1],
               {"vel": lax.rem(v + d, n_vel)})
        for d in range(1, n_vel)
    ]
    for copy in b1:
        copy.start()
    for d in range(1, n_vel):
        b1[d - 1].wait_recv()
        packed = packed + ld_rv[d - 1]
    ld_sec[...] = packed
    b2 = [
        remote(ld_sec, ld_rs.at[d - 1], b2_send.at[d - 1], b2_recv.at[d - 1],
               {"sec": lax.rem(s + d, n_sec)})
        for d in range(1, n_sec)
    ]
    for copy in b2:
        copy.start()
    for d in range(1, n_sec):
        b2[d - 1].wait_recv()
        packed = packed + ld_rs[d - 1]

    signed = cols[24:32, :]
    loaded = cols[32:40, :] * packed

    def everything(value):
        return jnp.sum(jnp.sum(value, axis=0, keepdims=True), axis=1, keepdims=True)

    shift_mass = jnp.zeros((1, 1), jnp.float32)
    shift_flow = jnp.zeros((1, 1), jnp.float32)
    for turn in range(NEWTON):
        if turn == 0:
            scaled = loaded
            miss_mass, miss_flow = -goal[0], -goal[1]
        else:
            growth = jnp.exp(shift_mass + shift_flow * signed)
            scaled = loaded * growth
            excess = loaded * (growth - 1.0)
            miss_mass = everything(excess) - goal[0]
            miss_flow = everything(excess * signed) - goal[1]
        m0 = everything(scaled)
        m1 = everything(scaled * signed)
        m2 = everything(scaled * signed * signed)
        determinant = m0 * m2 - m1 * m1
        new_mass = shift_mass - (m2 * miss_mass - m1 * miss_flow) / determinant
        shift_flow = shift_flow - (m0 * miss_flow - m1 * miss_mass) / determinant
        shift_mass = new_mass
    grow_out[...] = jnp.exp(shift_mass + shift_flow * column(6)) - 1.0

    for c in range(CHUNKS):
        stores[c].wait()

        @pl.when(s < n_sec - 1)
        def _():
            pos_copy(c).wait_send()

        @pl.when(s > 0)
        def _():
            neg_copy(c).wait_send()

    for d in range(1, n_vel):
        when_owner(lax.rem(v + d, n_vel), lambda: a1(d).wait_send())
        when_owner(v, lambda: a3(d, mine, lax.rem(v + d, n_vel)).wait_send())
        b1[d - 1].wait_send()
    for d in range(1, n_sec):
        pb_copy(d).wait_send()
        when_owner(v, lambda: a2(d, s, lax.rem(s + d, n_sec)).wait_send())
        b2[d - 1].wait_send()


def body(n_sec, n_vel, distribution, collision, lower_blocks, upper_blocks, diag_inverse):
    nodes, cells = distribution.shape
    length = cells // TUBES
    rows = nodes // NXI
    pairs = rows // 2
    slices = 4 * length
    total = n_sec * length
    row_table, col_table = tables()
    f32 = jnp.float32
    vmem = pl.BlockSpec(memory_space=pltpu.VMEM)
    dma = pltpu.SemaphoreType.DMA
    syn, grow, macro = pl.pallas_call(
        functools.partial(kernel, n_sec, n_vel, length, rows),
        out_shape=(
            jax.ShapeDtypeStruct((nodes, cells), f32),
            jax.ShapeDtypeStruct((NXI, TUBES), f32),
            jax.ShapeDtypeStruct((5, cells), f32),
        ),
        in_specs=[
            pl.BlockSpec(memory_space=pltpu.SMEM), vmem, pl.BlockSpec(memory_space=pl.ANY),
            vmem, vmem, vmem, vmem,
        ],
        out_specs=(pl.BlockSpec(memory_space=pl.ANY), vmem, vmem),
        scratch_shapes=[
            pltpu.VMEM((nodes, cells), f32),
            pltpu.VMEM((nodes, cells), f32),
            pltpu.VMEM((pairs, 24, TUBES), f32),
            pltpu.VMEM((pairs, 24, TUBES), f32),
            pltpu.VMEM((pairs, 24, TUBES), f32),
            pltpu.VMEM((pairs, 24, TUBES), f32),
            pltpu.VMEM((slices, NXI, TUBES), f32),
            pltpu.VMEM((n_vel - 1, NXI, TUBES), f32),
            pltpu.VMEM((slices, n_sec, NXI, TUBES), f32),
            pltpu.VMEM((total * PROWS, TUBES), f32),
            pltpu.VMEM((5 * total, TUBES), f32),
            pltpu.VMEM((5 * total, TUBES), f32),
            pltpu.VMEM((5 * total, TUBES), f32),
            pltpu.VMEM((5 * total, TUBES), f32),
            pltpu.VMEM((4 * total, NXI, TUBES), f32),
            pltpu.VMEM((length * (length + 1), NXI, TUBES), f32),
            pltpu.VMEM((slices, NXI, TUBES), f32),
            pltpu.VMEM((8, TUBES), f32),
            pltpu.VMEM((8, TUBES), f32),
            pltpu.VMEM((n_vel - 1, 8, TUBES), f32),
            pltpu.VMEM((n_sec - 1, 8, TUBES), f32),
            dma,
            dma((CHUNKS,)), dma((CHUNKS,)), dma((CHUNKS,)), dma((CHUNKS,)), dma((CHUNKS,)),
            dma((n_vel - 1,)), dma((n_vel - 1,)),
            dma((n_sec - 1,)), dma((n_sec - 1,)),
            dma((n_vel - 1,)), dma((n_vel - 1,)),
            dma((n_sec - 1,)), dma((n_sec - 1,)),
            dma((n_vel - 1,)), dma((n_vel - 1,)),
            dma((n_sec - 1,)), dma((n_sec - 1,)),
        ],
        compiler_params=pltpu.CompilerParams(
            collective_id=0, has_side_effects=True, vmem_limit_bytes=40 * 1024 * 1024
        ),
    )(
        jnp.asarray(row_table), jnp.asarray(col_table), distribution,
        collision.reshape(1, cells), lower_blocks, upper_blocks, diag_inverse,
    )
    field = syn.reshape(rows, NXI, cells)
    new = field + jnp.abs(field) * grow[None, :, 0:1]
    return (new.reshape(nodes, cells), macro)


def solution(mesh):
    in_specs = (P("vel", "sec"), P("sec"), P(None, "sec"), P(None, "sec"), P(None, "sec"))
    out_specs = (P("vel", "sec"), P(None, "sec"))
    run = functools.partial(body, mesh.shape["sec"], mesh.shape["vel"])
    return jax.shard_map(run, mesh=mesh, in_specs=in_specs, out_specs=out_specs, check_vma=False)
```

```python
import functools
import math

import jax
import jax.numpy as jnp
import numpy as np
from jax import lax
from jax.experimental import pallas as pl
from jax.experimental.pallas import tpu as pltpu
from jax.sharding import PartitionSpec as P

NXI = 24
TUBES = 128
JACOBI = 4
NEWTON = 2
CHUNKS = 6
PROWS = 80
pseudo_rate = 1.0
MESH = pl.DeviceIdType.MESH


def hermite_rule(count):
    quarter = math.pi ** (-0.25)
    found = []
    last_slope = 1.0
    for index in range(count // 2):
        if index == 0:
            guess = math.sqrt(2.0 * count + 1.0) - 1.85575 * (2.0 * count + 1.0) ** (-0.16667)
        elif index == 1:
            guess = guess - 1.14 * count**0.426 / guess
        elif index == 2:
            guess = 1.86 * guess - 0.86 * found[0][0]
        elif index == 3:
            guess = 1.91 * guess - 0.91 * found[1][0]
        else:
            guess = 2.0 * guess - found[index - 2][0]
        for repeat in range(60):
            current = quarter
            previous = 0.0
            for order in range(count):
                older = previous
                previous = current
                current = (
                    guess * math.sqrt(2.0 / (order + 1)) * previous
                    - math.sqrt(order / (order + 1.0)) * older
                )
            last_slope = math.sqrt(2.0 * count) * previous
            guess = guess - current / last_slope
        found.append((guess, 2.0 / (last_slope * last_slope)))
    positive = found[::-1]
    points = [-pair[0] for pair in found] + [pair[0] for pair in positive]
    weights = [pair[1] for pair in found] + [pair[1] for pair in positive]
    return (np.array(points), np.array(weights))


def tables():
    points, weights = hermite_rule(NXI)
    h = weights / math.sqrt(math.pi)
    y = np.repeat(points, NXI)
    z = np.tile(points, NXI)
    g = np.repeat(h, NXI) * np.tile(h, NXI)
    e = y * y + z * z - 1.0
    rows = np.concatenate([g, g * y, g * z, g * e, y, z, e]).astype(np.float32)
    cols = np.zeros((40, 128))
    x = points
    listed = [np.abs(x), 2.0 * x, (x * x - 0.5) / 1.5, h, h * x, h * (x * x - 0.5), x]
    for k, column in enumerate(listed):
        cols[:24, k] = column
    for lane in range(3):
        cols[24:32, lane] = x[lane * 8 : lane * 8 + 8]
        cols[32:40, lane] = h[lane * 8 : lane * 8 + 8]
    return rows, cols.astype(np.float32)


def kernel(
    n_sec, n_vel, length, rows,
    table_in, cols_in, dist, coll_in, lower_in, upper_in, diag_in,
    syn_out, grow_out, macro_out,
    table, cols, coll, lower, upper, diag, small_sem,
    dv, syn, out_p, out_n, in_p, in_n, s_part, s_recv, s_all, pb,
    om, hm, co, mac, t_all, w_tab, t_loc, ld_own, ld_sec, ld_rv, ld_rs,
    dist_sem, syn_sem, p_send, p_recv, n_send, n_recv,
    a1_send, a1_recv, a2_send, a2_recv, a3_send, a3_recv,
    pb_send, pb_recv, b1_send, b1_recv, b2_send, b2_recv,
):
    s = lax.axis_index("sec")
    v = lax.axis_index("vel")
    total = n_sec * length
    slices = 4 * length
    pairs = rows // 2
    per = pairs // CHUNKS
    all_rows = NXI * NXI

    load = pltpu.make_async_copy(dist, dv, dist_sem)
    small = [
        pltpu.make_async_copy(src, dst, small_sem.at[k])
        for k, (src, dst) in enumerate(
            (
                (cols_in, cols), (coll_in, coll), (table_in, table),
                (lower_in, lower), (upper_in, upper), (diag_in, diag),
            )
        )
    ]
    for copy in small[:3]:
        copy.start()
    load.start()
    for copy in small[3:]:
        copy.start()
    barrier = pltpu.get_barrier_semaphore()
    for d in range(1, n_vel):
        pl.semaphore_signal(
            barrier, inc=1, device_id={"vel": lax.rem(v + d, n_vel)}, device_id_type=MESH
        )
    for d in range(1, n_sec):
        pl.semaphore_signal(
            barrier, inc=1, device_id={"sec": lax.rem(s + d, n_sec)}, device_id_type=MESH
        )

    def remote(src, dst, send, recv, where):
        return pltpu.make_async_remote_copy(
            src_ref=src, dst_ref=dst, send_sem=send, recv_sem=recv,
            device_id=where, device_id_type=MESH,
        )

    def column(k):
        return jnp.broadcast_to(cols[0:24, k : k + 1], (24, TUBES))

    small[0].wait()
    small[1].wait()
    sub = lax.broadcasted_iota(jnp.int32, (8, TUBES), 0)
    low = sub < 4
    pos = lax.broadcasted_iota(jnp.int32, (24, TUBES), 0) >= 12
    reach = column(0) * float(total)

    inv, rate = [], []
    for p in range(length):
        den = reach + coll[0:1, p * TUBES : (p + 1) * TUBES] + pseudo_rate
        i = 1.0 / den
        inv.append(i)
        rate.append(reach * i)
    zero = jnp.zeros((24, TUBES), jnp.float32)
    w = [[zero] * length for _ in range(length)]
    a = [zero] * length
    fw = None
    for p in range(length):
        row = [rate[p] * e for e in fw[0]] + [inv[p]] if fw else [inv[p]]
        carry = rate[p] * fw[1] if fw else rate[p]
        fw = (row, carry)
        for q in range(p + 1):
            w[p][q] = jnp.where(pos, row[q], w[p][q])
        a[p] = jnp.where(pos, carry, a[p])
    bw = None
    for p in reversed(range(length)):
        row = [inv[p]] + [rate[p] * e for e in bw[0]] if bw else [inv[p]]
        carry = rate[p] * bw[1] if bw else rate[p]
        bw = (row, carry)
        for k in range(len(row)):
            w[p][p + k] = jnp.where(pos, w[p][p + k], row[k])
        a[p] = jnp.where(pos, a[p], carry)
    for p in range(length):
        for q in range(length):
            w_tab[p * (length + 1) + q] = w[p][q]
        w_tab[p * (length + 1) + length] = a[p]
    last = [jnp.where(pos, w[length - 1][q], w[0][q]) for q in range(length)]
    through = jnp.where(pos, a[length - 1], a[0])
    mix = through[8:16]
    mix_r = pltpu.roll(mix, 4, 0)
    thr_n = jnp.concatenate([through[0:8], through[0:8], jnp.where(low, mix, mix_r)], axis=0)
    thr_p = jnp.concatenate([through[16:24], through[16:24], jnp.where(low, mix_r, mix)], axis=0)

    @pl.when(s == 0)
    def _():
        in_p[...] = jnp.zeros_like(in_p)

    @pl.when(s == n_sec - 1)
    def _():
        in_n[...] = jnp.zeros_like(in_n)

    pl.semaphore_wait(barrier, n_vel + n_sec - 2)
    small[2].wait()
    load.wait()

    def chunk(c):
        return pl.ds(c * per, per)

    def pos_copy(c):
        to = jnp.minimum(s + 1, n_sec - 1)
        return remote(out_p.at[chunk(c)], in_p.at[chunk(c)], p_send.at[c], p_recv.at[c], {"sec": to})

    def neg_copy(c):
        to = jnp.maximum(s - 1, 0)
        return remote(out_n.at[chunk(c)], in_n.at[chunk(c)], n_send.at[c], n_recv.at[c], {"sec": to})

    def first_pass(k, acc):
        acc = list(acc)
        bs = []
        for half in range(2):
            r = 2 * k + half
            at = v * rows + r
            d = [
                dv[pl.ds(pl.multiple_of(k * 48, 8) + half * 24, 24), p * TUBES : (p + 1) * TUBES]
                for p in range(length)
            ]
            for q in range(4):
                scale = table[q * all_rows + at]
                for p in range(length):
                    acc[p * 4 + q] = acc[p * 4 + q] + scale * d[p]
            b = last[0] * d[0]
            for p in range(1, length):
                b = b + last[p] * d[p]
            bs.append(b)
        b0, b1 = bs
        out_n[k, 0:8] = b0[0:8]
        out_n[k, 8:16] = b1[0:8]
        out_n[k, 16:24] = jnp.where(low, b0[8:16], pltpu.roll(b1[8:16], 4, 0))
        out_p[k, 0:8] = b0[16:24]
        out_p[k, 8:16] = b1[16:24]
        out_p[k, 16:24] = jnp.where(low, pltpu.roll(b0[8:16], 4, 0), b1[8:16])
        return tuple(acc)

    acc = (zero,) * slices
    for c in range(CHUNKS):
        acc = lax.fori_loop(c * per, (c + 1) * per, first_pass, acc)

        @pl.when(s == 0)
        def _():
            pos_copy(c).start()

        @pl.when(s == n_sec - 1)
        def _():
            neg_copy(c).start()

    for k in range(slices):
        s_part[k] = acc[k]

    def when_owner(index, run):
        if n_vel == slices:
            run()
        else:
            pl.when(index < slices)(run)

    def a1(d):
        to = lax.rem(v + d, n_vel)
        slot = jnp.minimum(to, slices - 1)
        return remote(s_part.at[slot], s_recv.at[d - 1], a1_send.at[d - 1], a1_recv.at[d - 1], {"vel": to})

    for d in range(1, n_vel):
        when_owner(lax.rem(v + d, n_vel), lambda: a1(d).start())

    for copy in small[3:]:
        copy.wait()
    for p in range(length):
        lanes = slice(p * TUBES, (p + 1) * TUBES)
        base = (s * length + p) * PROWS
        for k, block in enumerate((lower, upper, diag)):
            for e in range(25):
                pb[pl.ds(base + k * 25 + e, 1), :] = block[e : e + 1, lanes]
        pb[pl.ds(base + 75, 1), :] = coll[0:1, lanes]
    own = pl.ds(s * length * PROWS, length * PROWS)

    def pb_copy(d):
        to = lax.rem(s + d, n_sec)
        return remote(pb.at[own], pb.at[own], pb_send.at[d - 1], pb_recv.at[d - 1], {"sec": to})

    def pb_wait(d):
        frm = lax.rem(s + n_sec - d, n_sec)
        there = pl.ds(frm * length * PROWS, length * PROWS)
        remote(pb.at[there], pb.at[there], pb_send.at[d - 1], pb_recv.at[d - 1], {"sec": frm}).wait_recv()

    for d in range(1, n_sec):
        pb_copy(d).start()

    mine = jnp.minimum(v, slices - 1)

    def a2(d, slot, to):
        return remote(
            s_all.at[mine, slot], s_all.at[mine, slot], a2_send.at[d - 1], a2_recv.at[d - 1], {"sec": to}
        )

    def reduce_slices():
        got = s_part[mine]
        for d in range(1, n_vel):
            a1(d).wait_recv()
            got = got + s_recv[d - 1]
        s_all[mine, s] = got
        for d in range(1, n_sec):
            a2(d, s, lax.rem(s + d, n_sec)).start()

    when_owner(v, reduce_slices)

    def relay(c):
        def forward_pos():
            pos_copy(c).wait_recv()

            @pl.when(s < n_sec - 1)
            def _():
                out_p[chunk(c)] = out_p[chunk(c)] + thr_p[None] * in_p[chunk(c)]
                pos_copy(c).start()

        def forward_neg():
            neg_copy(c).wait_recv()

            @pl.when(s > 0)
            def _():
                out_n[chunk(c)] = out_n[chunk(c)] + thr_n[None] * in_n[chunk(c)]
                neg_copy(c).start()

        @pl.when(s < n_sec // 2)
        def _():
            pl.when(s > 0)(forward_pos)
            forward_neg()

        @pl.when(s >= n_sec // 2)
        def _():
            pl.when(s < n_sec - 1)(forward_neg)
            forward_pos()

    def a3(d, slot, to):
        return remote(s_all.at[slot], s_all.at[slot], a3_send.at[d - 1], a3_recv.at[d - 1], {"vel": to})

    def gather_slices():
        for d in range(1, n_sec):
            frm = lax.rem(s + n_sec - d, n_sec)
            a2(d, frm, frm).wait_recv()
        for d in range(1, n_vel):
            a3(d, mine, lax.rem(v + d, n_vel)).start()

    when_owner(v, gather_slices)
    inner = jnp.logical_and(s > 0, s < n_sec - 1)

    @pl.when(inner)
    def _():
        for c in range(CHUNKS):
            relay(c)

    for d in range(1, n_vel):
        frm = lax.rem(v + n_vel - d, n_vel)
        when_owner(frm, lambda: a3(d, jnp.minimum(frm, slices - 1), frm).wait_recv())
    for d in range(1, n_sec):
        pb_wait(d)

    hx, hxx, hxe = column(3), column(4), column(5)
    x2, en = column(1), column(2)

    def total_of(value):
        return jnp.sum(value, axis=0, keepdims=True)

    for at in range(total):
        sec, p = at // length, at % length
        s0, s2, s3, s4 = [s_all[p * 4 + q, sec] for q in range(4)]
        om[0 * total + at : 0 * total + at + 1] = total_of(hx * s0)
        om[1 * total + at : 1 * total + at + 1] = total_of(hxx * s0)
        om[2 * total + at : 2 * total + at + 1] = total_of(hx * s2)
        om[3 * total + at : 3 * total + at + 1] = total_of(hx * s3)
        om[4 * total + at : 4 * total + at + 1] = total_of(hxe * s0 + hx * s4)

    thick, invs, rates = [], [], []
    for at in range(total):
        t = pb[at * PROWS + 75 : at * PROWS + 76]
        i = 1.0 / (reach + t + pseudo_rate)
        thick.append(t)
        invs.append(i)
        rates.append(reach * i)
    turned = [jnp.where(pos, rates[i], rates[total - 1 - i]) for i in range(total)]

    def sweep(drive):
        found, carried = [], None
        for i in range(total):
            here = jnp.where(pos, drive[i], drive[total - 1 - i])
            carried = here if carried is None else turned[i] * carried + here
            found.append(carried)
        return [jnp.where(pos, found[i], found[total - 1 - i]) for i in range(total)]

    halves = {}
    for q, norm in enumerate((1.0, 0.5, 0.5, 1.0)):
        goals, parts = [], []
        for at in range(total):
            m = [om[j * total + at : j * total + at + 1] for j in range(5)]
            if q == 0:
                goal = thick[at] * (m[0] + x2 * m[1] + en * m[4])
            elif q == 3:
                goal = jnp.broadcast_to(thick[at] * m[4] * (1.0 / 1.5), (24, TUBES))
            else:
                goal = jnp.broadcast_to(thick[at] * m[q + 1] * 2.0, (24, TUBES))
            sec, p = at // length, at % length
            goals.append(goal * invs[at])
            parts.append((s_all[p * 4 + q, sec] + norm * goal) * invs[at])
        swept = sweep(goals)
        for at in range(total):
            t_all[q * total + at] = swept[at]
        swept = sweep(parts)
        for at in range(total):
            f = swept[at]
            if q == 0:
                hm[at : at + 1] = total_of(hx * f)
                hm[total + at : total + at + 1] = total_of(hxx * f)
                halves[at] = hxe * f
            elif q == 3:
                hm[4 * total + at : 4 * total + at + 1] = total_of(halves[at] + hx * f)
            else:
                j = q + 1
                hm[j * total + at : j * total + at + 1] = total_of(hx * f)

    place = lax.broadcasted_iota(jnp.int32, (total, TUBES), 0)
    old = [om[j * total : (j + 1) * total] for j in range(5)]
    half = [hm[j * total : (j + 1) * total] for j in range(5)]
    resid = [half[j] - old[j] for j in range(5)]

    entries = [pb[pl.ds(e, total, stride=PROWS), :] for e in range(75)]

    def apply_block(first, vector):
        out = []
        for i in range(5):
            value = entries[first + i * 5] * vector[0]
            for j in range(1, 5):
                value = value + entries[first + i * 5 + j] * vector[j]
            out.append(value)
        return out

    corr = apply_block(50, resid)
    for _ in range(JACOBI):
        left = [jnp.where(place == 0, 0.0, pltpu.roll(c, 1, 0)) for c in corr]
        right = [jnp.where(place == total - 1, 0.0, pltpu.roll(c, total - 1, 0)) for c in corr]
        lo = apply_block(0, left)
        up = apply_block(25, right)
        corr = apply_block(50, [resid[j] - lo[j] - up[j] for j in range(5)])
    goal = []
    for j in range(5):
        macro = half[j] + corr[j]
        co[j * total : (j + 1) * total] = corr[j]
        mac[j * total : (j + 1) * total] = macro
        if j < 2:
            change = jnp.sum(old[j] - macro, axis=0, keepdims=True)
            goal.append(jnp.sum(change, axis=1, keepdims=True))
    for p in range(length):
        at = s * length + p
        c = [co[pl.ds(j * total + at, 1), :] for j in range(5)]
        for j in range(5):
            macro_out[j : j + 1, p * TUBES : (p + 1) * TUBES] = mac[pl.ds(j * total + at, 1), :]
        t_loc[p * 4 + 0] = t_all[0 * total + at] + (c[0] + x2 * c[1] + en * c[4])
        t_loc[p * 4 + 1] = t_all[1 * total + at] + 2.0 * c[2]
        t_loc[p * 4 + 2] = t_all[2 * total + at] + 2.0 * c[3]
        t_loc[p * 4 + 3] = t_all[3 * total + at] + c[4] * (1.0 / 1.5)

    @pl.when(jnp.logical_not(inner))
    def _():
        for c in range(CHUNKS):
            relay(c)

    def second_pass(k, acc):
        n_mix, p_mix = in_n[k, 16:24], in_p[k, 16:24]
        flow = (
            jnp.concatenate(
                [in_n[k, 0:8], jnp.where(low, n_mix, pltpu.roll(p_mix, 4, 0)), in_p[k, 0:8]], axis=0
            ),
            jnp.concatenate(
                [in_n[k, 8:16], jnp.where(low, pltpu.roll(n_mix, 4, 0), p_mix), in_p[k, 8:16]], axis=0
            ),
        )
        for half_row in range(2):
            at = v * rows + 2 * k + half_row
            here = pl.ds(pl.multiple_of(k * 48, 8) + half_row * 24, 24)
            g = table[at]
            y = table[4 * all_rows + at]
            z = table[5 * all_rows + at]
            e = table[6 * all_rows + at]
            d = [dv[here, p * TUBES : (p + 1) * TUBES] for p in range(length)]
            size = None
            for p in range(length):
                f = t_loc[p * 4] + y * t_loc[p * 4 + 1] + z * t_loc[p * 4 + 2] + e * t_loc[p * 4 + 3]
                f = f + w_tab[p * (length + 1) + length] * flow[half_row]
                for q in range(length):
                    f = f + w_tab[p * (length + 1) + q] * d[q]
                syn[here, p * TUBES : (p + 1) * TUBES] = f
                size = jnp.abs(f) if size is None else size + jnp.abs(f)
            acc = acc + g * size
        return acc

    acc = zero
    stores = []
    for c in range(CHUNKS):
        acc = lax.fori_loop(c * per, (c + 1) * per, second_pass, acc)
        part = pl.ds(c * per * 48, per * 48)
        store = pltpu.make_async_copy(syn.at[part], syn_out.at[part], syn_sem.at[c])
        store.start()
        stores.append(store)

    lane = lax.broadcasted_iota(jnp.int32, (8, TUBES), 1)
    one = jnp.sum(acc, axis=1, keepdims=True)
    packed = jnp.where(lane == 0, one[0:8], jnp.where(lane == 1, one[8:16], one[16:24]))
    ld_own[...] = packed
    b1 = [
        remote(ld_own, ld_rv.at[d - 1], b1_send.at[d - 1], b1_recv.at[d - 1],
               {"vel": lax.rem(v + d, n_vel)})
        for d in range(1, n_vel)
    ]
    for copy in b1:
        copy.start()
    for d in range(1, n_vel):
        b1[d - 1].wait_recv()
        packed = packed + ld_rv[d - 1]
    ld_sec[...] = packed
    b2 = [
        remote(ld_sec, ld_rs.at[d - 1], b2_send.at[d - 1], b2_recv.at[d - 1],
               {"sec": lax.rem(s + d, n_sec)})
        for d in range(1, n_sec)
    ]
    for copy in b2:
        copy.start()
    for d in range(1, n_sec):
        b2[d - 1].wait_recv()
        packed = packed + ld_rs[d - 1]

    signed = cols[24:32, :]
    loaded = cols[32:40, :] * packed

    def everything(value):
        return jnp.sum(jnp.sum(value, axis=0, keepdims=True), axis=1, keepdims=True)

    shift_mass = jnp.zeros((1, 1), jnp.float32)
    shift_flow = jnp.zeros((1, 1), jnp.float32)
    for turn in range(NEWTON):
        if turn == 0:
            scaled = loaded
            miss_mass, miss_flow = -goal[0], -goal[1]
        else:
            growth = jnp.exp(shift_mass + shift_flow * signed)
            scaled = loaded * growth
            excess = loaded * (growth - 1.0)
            miss_mass = everything(excess) - goal[0]
            miss_flow = everything(excess * signed) - goal[1]
        m0 = everything(scaled)
        m1 = everything(scaled * signed)
        m2 = everything(scaled * signed * signed)
        determinant = m0 * m2 - m1 * m1
        new_mass = shift_mass - (m2 * miss_mass - m1 * miss_flow) / determinant
        shift_flow = shift_flow - (m0 * miss_flow - m1 * miss_mass) / determinant
        shift_mass = new_mass
    grow_out[...] = jnp.exp(shift_mass + shift_flow * column(6)) - 1.0

    for c in range(CHUNKS):
        stores[c].wait()

        @pl.when(s < n_sec - 1)
        def _():
            pos_copy(c).wait_send()

        @pl.when(s > 0)
        def _():
            neg_copy(c).wait_send()

    for d in range(1, n_vel):
        when_owner(lax.rem(v + d, n_vel), lambda: a1(d).wait_send())
        when_owner(v, lambda: a3(d, mine, lax.rem(v + d, n_vel)).wait_send())
        b1[d - 1].wait_send()
    for d in range(1, n_sec):
        pb_copy(d).wait_send()
        when_owner(v, lambda: a2(d, s, lax.rem(s + d, n_sec)).wait_send())
        b2[d - 1].wait_send()


def body(n_sec, n_vel, distribution, collision, lower_blocks, upper_blocks, diag_inverse):
    nodes, cells = distribution.shape
    length = cells // TUBES
    rows = nodes // NXI
    pairs = rows // 2
    slices = 4 * length
    total = n_sec * length
    row_table, col_table = tables()
    f32 = jnp.float32
    vmem = pl.BlockSpec(memory_space=pltpu.VMEM)
    dma = pltpu.SemaphoreType.DMA
    syn, grow, macro = pl.pallas_call(
        functools.partial(kernel, n_sec, n_vel, length, rows),
        out_shape=(
            jax.ShapeDtypeStruct((nodes, cells), f32),
            jax.ShapeDtypeStruct((NXI, TUBES), f32),
            jax.ShapeDtypeStruct((5, cells), f32),
        ),
        in_specs=[pl.BlockSpec(memory_space=pl.ANY)] * 7,
        out_specs=(pl.BlockSpec(memory_space=pl.ANY), vmem, vmem),
        scratch_shapes=[
            pltpu.SMEM(row_table.shape, f32),
            pltpu.VMEM(col_table.shape, f32),
            pltpu.VMEM((1, cells), f32),
            pltpu.VMEM((25, cells), f32),
            pltpu.VMEM((25, cells), f32),
            pltpu.VMEM((25, cells), f32),
            dma((6,)),
            pltpu.VMEM((nodes, cells), f32),
            pltpu.VMEM((nodes, cells), f32),
            pltpu.VMEM((pairs, 24, TUBES), f32),
            pltpu.VMEM((pairs, 24, TUBES), f32),
            pltpu.VMEM((pairs, 24, TUBES), f32),
            pltpu.VMEM((pairs, 24, TUBES), f32),
            pltpu.VMEM((slices, NXI, TUBES), f32),
            pltpu.VMEM((n_vel - 1, NXI, TUBES), f32),
            pltpu.VMEM((slices, n_sec, NXI, TUBES), f32),
            pltpu.VMEM((total * PROWS, TUBES), f32),
            pltpu.VMEM((5 * total, TUBES), f32),
            pltpu.VMEM((5 * total, TUBES), f32),
            pltpu.VMEM((5 * total, TUBES), f32),
            pltpu.VMEM((5 * total, TUBES), f32),
            pltpu.VMEM((4 * total, NXI, TUBES), f32),
            pltpu.VMEM((length * (length + 1), NXI, TUBES), f32),
            pltpu.VMEM((slices, NXI, TUBES), f32),
            pltpu.VMEM((8, TUBES), f32),
            pltpu.VMEM((8, TUBES), f32),
            pltpu.VMEM((n_vel - 1, 8, TUBES), f32),
            pltpu.VMEM((n_sec - 1, 8, TUBES), f32),
            dma,
            dma((CHUNKS,)), dma((CHUNKS,)), dma((CHUNKS,)), dma((CHUNKS,)), dma((CHUNKS,)),
            dma((n_vel - 1,)), dma((n_vel - 1,)),
            dma((n_sec - 1,)), dma((n_sec - 1,)),
            dma((n_vel - 1,)), dma((n_vel - 1,)),
            dma((n_sec - 1,)), dma((n_sec - 1,)),
            dma((n_vel - 1,)), dma((n_vel - 1,)),
            dma((n_sec - 1,)), dma((n_sec - 1,)),
        ],
        compiler_params=pltpu.CompilerParams(
            collective_id=0, has_side_effects=True, vmem_limit_bytes=56 * 1024 * 1024
        ),
    )(
        jnp.asarray(row_table), jnp.asarray(col_table), distribution,
        collision.reshape(1, cells), lower_blocks, upper_blocks, diag_inverse,
    )
    field = syn.reshape(rows, NXI, cells)
    new = field + jnp.abs(field) * grow[None, :, 0:1]
    return (new.reshape(nodes, cells), macro)


def solution(mesh):
    in_specs = (P("vel", "sec"), P("sec"), P(None, "sec"), P(None, "sec"), P(None, "sec"))
    out_specs = (P("vel", "sec"), P(None, "sec"))
    run = functools.partial(body, mesh.shape["sec"], mesh.shape["vel"])
    return jax.shard_map(run, mesh=mesh, in_specs=in_specs, out_specs=out_specs, check_vma=False)
```

```python
import functools
import math

import jax
import jax.numpy as jnp
import numpy as np
from jax import lax
from jax.experimental import pallas as pl
from jax.experimental.pallas import tpu as pltpu
from jax.sharding import PartitionSpec as P

NXI = 24
TUBES = 128
JACOBI = 4
NEWTON = 2
CHUNKS = 6
PROWS = 80
pseudo_rate = 1.0
MESH = pl.DeviceIdType.MESH


def hermite_rule(count):
    quarter = math.pi ** (-0.25)
    found = []
    last_slope = 1.0
    for index in range(count // 2):
        if index == 0:
            guess = math.sqrt(2.0 * count + 1.0) - 1.85575 * (2.0 * count + 1.0) ** (-0.16667)
        elif index == 1:
            guess = guess - 1.14 * count**0.426 / guess
        elif index == 2:
            guess = 1.86 * guess - 0.86 * found[0][0]
        elif index == 3:
            guess = 1.91 * guess - 0.91 * found[1][0]
        else:
            guess = 2.0 * guess - found[index - 2][0]
        for repeat in range(60):
            current = quarter
            previous = 0.0
            for order in range(count):
                older = previous
                previous = current
                current = (
                    guess * math.sqrt(2.0 / (order + 1)) * previous
                    - math.sqrt(order / (order + 1.0)) * older
                )
            last_slope = math.sqrt(2.0 * count) * previous
            guess = guess - current / last_slope
        found.append((guess, 2.0 / (last_slope * last_slope)))
    positive = found[::-1]
    points = [-pair[0] for pair in found] + [pair[0] for pair in positive]
    weights = [pair[1] for pair in found] + [pair[1] for pair in positive]
    return (np.array(points), np.array(weights))


def tables():
    points, weights = hermite_rule(NXI)
    h = weights / math.sqrt(math.pi)
    y = np.repeat(points, NXI)
    z = np.tile(points, NXI)
    g = np.repeat(h, NXI) * np.tile(h, NXI)
    e = y * y + z * z - 1.0
    rows = np.concatenate([g, g * y, g * z, g * e, y, z, e]).astype(np.float32)
    cols = np.zeros((40, 128))
    x = points
    listed = [np.abs(x), 2.0 * x, (x * x - 0.5) / 1.5, h, h * x, h * (x * x - 0.5), x]
    for k, column in enumerate(listed):
        cols[:24, k] = column
    for lane in range(3):
        cols[24:32, lane] = x[lane * 8 : lane * 8 + 8]
        cols[32:40, lane] = h[lane * 8 : lane * 8 + 8]
    return rows, cols.astype(np.float32)


def kernel(
    n_sec, n_vel, length, rows,
    table_in, cols_in, dist, coll_in, lower_in, upper_in, diag_in,
    syn_out, grow_out, macro_out,
    table, cols, coll, lower, upper, diag, small_sem,
    dv, syn, out_p, out_n, in_p, in_n, s_part, s_recv, s_all, pb,
    om, hm, co, mac, t_all, w_tab, t_loc, ld_own, ld_sec, ld_rv, ld_rs,
    dist_sem, syn_sem, p_send, p_recv, n_send, n_recv,
    a1_send, a1_recv, a2_send, a2_recv, a3_send, a3_recv,
    pb_send, pb_recv, b1_send, b1_recv, b2_send, b2_recv,
    tmp_a, tmp_b, thr_own, thr_side, y_send, ta_recv, tb_recv, th_send, th_recv, px_send, px_recv,
):
    s = lax.axis_index("sec")
    v = lax.axis_index("vel")
    total = n_sec * length
    slices = 4 * length
    pairs = rows // 2
    per = pairs // CHUNKS
    all_rows = NXI * NXI

    load = pltpu.make_async_copy(dist, dv, dist_sem)
    small = [
        pltpu.make_async_copy(src, dst, small_sem.at[k])
        for k, (src, dst) in enumerate(
            (
                (cols_in, cols), (coll_in, coll), (table_in, table),
                (lower_in, lower), (upper_in, upper), (diag_in, diag),
            )
        )
    ]
    for copy in small[:3]:
        copy.start()
    load.start()
    for copy in small[3:]:
        copy.start()
    barrier = pltpu.get_barrier_semaphore()
    for d in range(1, n_vel):
        pl.semaphore_signal(
            barrier, inc=1, device_id={"vel": lax.rem(v + d, n_vel)}, device_id_type=MESH
        )
    for d in range(1, n_sec):
        pl.semaphore_signal(
            barrier, inc=1, device_id={"sec": lax.rem(s + d, n_sec)}, device_id_type=MESH
        )

    def remote(src, dst, send, recv, where):
        return pltpu.make_async_remote_copy(
            src_ref=src, dst_ref=dst, send_sem=send, recv_sem=recv,
            device_id=where, device_id_type=MESH,
        )

    def column(k):
        return jnp.broadcast_to(cols[0:24, k : k + 1], (24, TUBES))

    small[0].wait()
    small[1].wait()
    sub = lax.broadcasted_iota(jnp.int32, (8, TUBES), 0)
    low = sub < 4
    pos = lax.broadcasted_iota(jnp.int32, (24, TUBES), 0) >= 12
    reach = column(0) * float(total)

    inv, rate = [], []
    for p in range(length):
        den = reach + coll[0:1, p * TUBES : (p + 1) * TUBES] + pseudo_rate
        i = 1.0 / den
        inv.append(i)
        rate.append(reach * i)
    zero = jnp.zeros((24, TUBES), jnp.float32)
    w = [[zero] * length for _ in range(length)]
    a = [zero] * length
    fw = None
    for p in range(length):
        row = [rate[p] * e for e in fw[0]] + [inv[p]] if fw else [inv[p]]
        carry = rate[p] * fw[1] if fw else rate[p]
        fw = (row, carry)
        for q in range(p + 1):
            w[p][q] = jnp.where(pos, row[q], w[p][q])
        a[p] = jnp.where(pos, carry, a[p])
    bw = None
    for p in reversed(range(length)):
        row = [inv[p]] + [rate[p] * e for e in bw[0]] if bw else [inv[p]]
        carry = rate[p] * bw[1] if bw else rate[p]
        bw = (row, carry)
        for k in range(len(row)):
            w[p][p + k] = jnp.where(pos, w[p][p + k], row[k])
        a[p] = jnp.where(pos, a[p], carry)
    for p in range(length):
        for q in range(length):
            w_tab[p * (length + 1) + q] = w[p][q]
        w_tab[p * (length + 1) + length] = a[p]
    last = [jnp.where(pos, w[length - 1][q], w[0][q]) for q in range(length)]
    through = jnp.where(pos, a[length - 1], a[0])
    mix = through[8:16]
    mix_r = pltpu.roll(mix, 4, 0)
    thr_n = jnp.concatenate([through[0:8], through[0:8], jnp.where(low, mix, mix_r)], axis=0)
    thr_p = jnp.concatenate([through[16:24], through[16:24], jnp.where(low, mix_r, mix)], axis=0)

    @pl.when(s == 0)
    def _():
        in_p[...] = jnp.zeros_like(in_p)

    @pl.when(s == n_sec - 1)
    def _():
        in_n[...] = jnp.zeros_like(in_n)

    pl.semaphore_wait(barrier, n_vel + n_sec - 2)
    small[2].wait()
    load.wait()

    def chunk(c):
        return pl.ds(c * per, per)

    def pos_copy(c):
        to = jnp.minimum(s + 1, n_sec - 1)
        return remote(out_p.at[chunk(c)], in_p.at[chunk(c)], p_send.at[c], p_recv.at[c], {"sec": to})

    def neg_copy(c):
        to = jnp.maximum(s - 1, 0)
        return remote(out_n.at[chunk(c)], in_n.at[chunk(c)], n_send.at[c], n_recv.at[c], {"sec": to})

    square = n_sec == 4
    outs, ins, thrs = (out_p, out_n), (in_p, in_n), (thr_p, thr_n)
    x_sends, in_recvs = (p_send, n_send), (p_recv, n_recv)

    def device_of(way, role):
        return role if way == 0 else 3 - role

    def when_role(way, role, run):
        pl.when(s == device_of(way, role))(run)

    def out_to(way, c, role):
        return remote(outs[way].at[chunk(c)], ins[way].at[chunk(c)], x_sends[way].at[c],
                      in_recvs[way].at[c], {"sec": device_of(way, role)})

    def out_to_a(way, c, role):
        return remote(outs[way].at[chunk(c)], tmp_a.at[way, chunk(c)], x_sends[way].at[c],
                      ta_recv.at[way, c], {"sec": device_of(way, role)})

    def out_to_b(way, c, role):
        return remote(outs[way].at[chunk(c)], tmp_b.at[way, chunk(c)], x_sends[way].at[c],
                      tb_recv.at[way, c], {"sec": device_of(way, role)})

    def a_to(way, c, role):
        return remote(tmp_a.at[way, chunk(c)], ins[way].at[chunk(c)], y_send.at[way, c],
                      in_recvs[way].at[c], {"sec": device_of(way, role)})

    def b_to(way, c, role):
        return remote(tmp_b.at[way, chunk(c)], ins[way].at[chunk(c)], x_sends[way].at[c],
                      in_recvs[way].at[c], {"sec": device_of(way, role)})

    def thr_to(way, role):
        return remote(thr_own.at[way], thr_side.at[way], th_send.at[way],
                      th_recv.at[way], {"sec": device_of(way, role)})

    if square:
        for way in range(2):
            thr_own[way] = thrs[way]
            when_role(way, 1, lambda: thr_to(way, 0).start())
            when_role(way, 2, lambda: thr_to(way, 3).start())

    def launch(way, c):
        when_role(way, 0, lambda: out_to(way, c, 1).start())
        if c % 2 == 0:
            when_role(way, 1, lambda: out_to_a(way, c, 0).start())
        else:
            when_role(way, 2, lambda: out_to_a(way, c, 3).start())

    def near_job(way, i):
        even, odd = 2 * i, 2 * i + 1

        def role_0():
            if i == 0:
                thr_to(way, 1).wait_recv()
            out_to_a(way, even, 1).wait_recv()
            tmp_a[way, chunk(even)] = (
                thr_side[way][None] * outs[way][chunk(even)] + tmp_a[way, chunk(even)]
            )
            a_to(way, even, 2).start()

        def role_1():
            out_to(way, odd, 0).wait_recv()
            outs[way][chunk(odd)] = outs[way][chunk(odd)] + thrs[way][None] * ins[way][chunk(odd)]
            out_to_b(way, odd, 3).start()

        when_role(way, 0, role_0)
        when_role(way, 1, role_1)

    def far_job(way, i):
        even, odd = 2 * i, 2 * i + 1

        def role_2():
            out_to(way, even, 3).wait_recv()
            outs[way][chunk(even)] = outs[way][chunk(even)] + thrs[way][None] * ins[way][chunk(even)]
            out_to(way, even, 3).start()

        def role_3():
            if i == 0:
                thr_to(way, 2).wait_recv()
            out_to_b(way, odd, 1).wait_recv()
            b_to(way, odd, 2).start()
            out_to_a(way, odd, 2).wait_recv()
            ins[way][chunk(odd)] = (
                thr_side[way][None] * tmp_b[way, chunk(odd)] + tmp_a[way, chunk(odd)]
            )

        when_role(way, 2, role_2)
        when_role(way, 3, role_3)

    def last_waits(way):
        def even_in():
            for c in range(0, CHUNKS, 2):
                out_to(way, c, 2).wait_recv()

        def odd_in():
            for c in range(1, CHUNKS, 2):
                out_to(way, c, 3).wait_recv()

        when_role(way, 1, even_in)
        when_role(way, 2, odd_in)
        when_role(way, 3, even_in)

    def sent(way, c):
        when_role(way, 0, lambda: out_to(way, c, 1).wait_send())
        if c % 2 == 0:
            when_role(way, 0, lambda: a_to(way, c, 2).wait_send())
            when_role(way, 1, lambda: out_to_a(way, c, 0).wait_send())
            when_role(way, 2, lambda: out_to(way, c, 3).wait_send())
        else:
            when_role(way, 1, lambda: out_to_b(way, c, 3).wait_send())
            when_role(way, 2, lambda: out_to_a(way, c, 3).wait_send())
            when_role(way, 3, lambda: b_to(way, c, 2).wait_send())

    def first_pass(k, acc):
        acc = list(acc)
        bs = []
        for half in range(2):
            r = 2 * k + half
            at = v * rows + r
            d = [
                dv[pl.ds(pl.multiple_of(k * 48, 8) + half * 24, 24), p * TUBES : (p + 1) * TUBES]
                for p in range(length)
            ]
            for q in range(4):
                scale = table[q * all_rows + at]
                for p in range(length):
                    acc[p * 4 + q] = acc[p * 4 + q] + scale * d[p]
            b = last[0] * d[0]
            for p in range(1, length):
                b = b + last[p] * d[p]
            bs.append(b)
        b0, b1 = bs
        out_n[k, 0:8] = b0[0:8]
        out_n[k, 8:16] = b1[0:8]
        out_n[k, 16:24] = jnp.where(low, b0[8:16], pltpu.roll(b1[8:16], 4, 0))
        out_p[k, 0:8] = b0[16:24]
        out_p[k, 8:16] = b1[16:24]
        out_p[k, 16:24] = jnp.where(low, pltpu.roll(b0[8:16], 4, 0), b1[8:16])
        return tuple(acc)

    acc = (zero,) * slices
    for c in range(CHUNKS):
        acc = lax.fori_loop(c * per, (c + 1) * per, first_pass, acc)
        if square:
            launch(0, c)
            launch(1, c)
            continue

        @pl.when(s == 0)
        def _():
            pos_copy(c).start()

        @pl.when(s == n_sec - 1)
        def _():
            neg_copy(c).start()

    for k in range(slices):
        s_part[k] = acc[k]

    def when_owner(index, run):
        if n_vel == slices:
            run()
        else:
            pl.when(index < slices)(run)

    def a1(d):
        to = lax.rem(v + d, n_vel)
        slot = jnp.minimum(to, slices - 1)
        return remote(s_part.at[slot], s_recv.at[d - 1], a1_send.at[d - 1], a1_recv.at[d - 1], {"vel": to})

    for d in range(1, n_vel):
        when_owner(lax.rem(v + d, n_vel), lambda: a1(d).start())

    for copy in small[3:]:
        copy.wait()
    for p in range(length):
        lanes = slice(p * TUBES, (p + 1) * TUBES)
        base = (s * length + p) * PROWS
        for k, block in enumerate((lower, upper, diag)):
            for e in range(25):
                pb[pl.ds(base + k * 25 + e, 1), :] = block[e : e + 1, lanes]
        pb[pl.ds(base + 75, 1), :] = coll[0:1, lanes]
    core = lax.rem(v, 2)
    share = length * PROWS // 2

    def half_of(sec, which):
        return pl.ds((sec * 2 + which) * share, share)

    def pb_copy(d):
        to = lax.rem(s + d, n_sec)
        mine_rows = pb.at[half_of(s, core)]
        return remote(mine_rows, mine_rows, pb_send.at[d - 1], pb_recv.at[d - 1], {"sec": to})

    def pb_wait(d):
        frm = lax.rem(s + n_sec - d, n_sec)
        there = pb.at[half_of(frm, core)]
        remote(there, there, pb_send.at[d - 1], pb_recv.at[d - 1], {"sec": frm}).wait_recv()

    def pb_cross(d, other=0):
        frm = lax.rem(s + n_sec - d, n_sec)
        there = pb.at[half_of(frm, core + other * (1 - 2 * core))]
        return remote(there, there, px_send.at[d - 1], px_recv.at[d - 1], {"vel": v + 1 - 2 * core})

    for d in range(1, n_sec):
        pb_copy(d).start()

    mine = jnp.minimum(v, slices - 1)

    def a2(d, slot, to):
        return remote(
            s_all.at[mine, slot], s_all.at[mine, slot], a2_send.at[d - 1], a2_recv.at[d - 1], {"sec": to}
        )

    def reduce_slices():
        got = s_part[mine]
        for d in range(1, n_vel):
            a1(d).wait_recv()
            got = got + s_recv[d - 1]
        s_all[mine, s] = got
        for d in range(1, n_sec):
            a2(d, s, lax.rem(s + d, n_sec)).start()

    when_owner(v, reduce_slices)

    def relay(c):
        def forward_pos():
            pos_copy(c).wait_recv()

            @pl.when(s < n_sec - 1)
            def _():
                out_p[chunk(c)] = out_p[chunk(c)] + thr_p[None] * in_p[chunk(c)]
                pos_copy(c).start()

        def forward_neg():
            neg_copy(c).wait_recv()

            @pl.when(s > 0)
            def _():
                out_n[chunk(c)] = out_n[chunk(c)] + thr_n[None] * in_n[chunk(c)]
                neg_copy(c).start()

        @pl.when(s < n_sec // 2)
        def _():
            pl.when(s > 0)(forward_pos)
            forward_neg()

        @pl.when(s >= n_sec // 2)
        def _():
            pl.when(s < n_sec - 1)(forward_neg)
            forward_pos()

    def a3(d, slot, to):
        return remote(s_all.at[slot], s_all.at[slot], a3_send.at[d - 1], a3_recv.at[d - 1], {"vel": to})

    def gather_slices():
        for d in range(1, n_sec):
            frm = lax.rem(s + n_sec - d, n_sec)
            a2(d, frm, frm).wait_recv()
        for d in range(1, n_vel):
            a3(d, mine, lax.rem(v + d, n_vel)).start()

    when_owner(v, gather_slices)
    inner = jnp.logical_and(s > 0, s < n_sec - 1)

    if square:
        steps = CHUNKS // 2

        def jobs(first, second):
            for i in range(steps + 1):
                if i < steps:
                    near_job(first, i)
                if i > 0:
                    far_job(second, i - 1)

        pl.when(s < 2)(lambda: jobs(0, 1))
        pl.when(s >= 2)(lambda: jobs(1, 0))
    else:

        @pl.when(inner)
        def _():
            for c in range(CHUNKS):
                relay(c)

    for d in range(1, n_sec):
        pb_wait(d)
        pb_cross(d).start()
    for d in range(1, n_vel):
        frm = lax.rem(v + n_vel - d, n_vel)
        when_owner(frm, lambda: a3(d, jnp.minimum(frm, slices - 1), frm).wait_recv())
    for d in range(1, n_sec):
        pb_cross(d, 1).wait_recv()

    hx, hxx, hxe = column(3), column(4), column(5)
    x2, en = column(1), column(2)

    def total_of(value):
        return jnp.sum(value, axis=0, keepdims=True)

    for at in range(total):
        sec, p = at // length, at % length
        s0, s2, s3, s4 = [s_all[p * 4 + q, sec] for q in range(4)]
        om[0 * total + at : 0 * total + at + 1] = total_of(hx * s0)
        om[1 * total + at : 1 * total + at + 1] = total_of(hxx * s0)
        om[2 * total + at : 2 * total + at + 1] = total_of(hx * s2)
        om[3 * total + at : 3 * total + at + 1] = total_of(hx * s3)
        om[4 * total + at : 4 * total + at + 1] = total_of(hxe * s0 + hx * s4)

    thick, invs, rates = [], [], []
    for at in range(total):
        t = pb[at * PROWS + 75 : at * PROWS + 76]
        i = 1.0 / (reach + t + pseudo_rate)
        thick.append(t)
        invs.append(i)
        rates.append(reach * i)
    turned = [jnp.where(pos, rates[i], rates[total - 1 - i]) for i in range(total)]

    def sweep(drive):
        found, carried = [], None
        for i in range(total):
            here = jnp.where(pos, drive[i], drive[total - 1 - i])
            carried = here if carried is None else turned[i] * carried + here
            found.append(carried)
        return [jnp.where(pos, found[i], found[total - 1 - i]) for i in range(total)]

    halves = {}
    for q, norm in enumerate((1.0, 0.5, 0.5, 1.0)):
        goals, parts = [], []
        for at in range(total):
            m = [om[j * total + at : j * total + at + 1] for j in range(5)]
            if q == 0:
                goal = thick[at] * (m[0] + x2 * m[1] + en * m[4])
            elif q == 3:
                goal = jnp.broadcast_to(thick[at] * m[4] * (1.0 / 1.5), (24, TUBES))
            else:
                goal = jnp.broadcast_to(thick[at] * m[q + 1] * 2.0, (24, TUBES))
            sec, p = at // length, at % length
            goals.append(goal * invs[at])
            parts.append((s_all[p * 4 + q, sec] + norm * goal) * invs[at])
        swept = sweep(goals)
        for at in range(total):
            t_all[q * total + at] = swept[at]
        swept = sweep(parts)
        for at in range(total):
            f = swept[at]
            if q == 0:
                hm[at : at + 1] = total_of(hx * f)
                hm[total + at : total + at + 1] = total_of(hxx * f)
                halves[at] = hxe * f
            elif q == 3:
                hm[4 * total + at : 4 * total + at + 1] = total_of(halves[at] + hx * f)
            else:
                j = q + 1
                hm[j * total + at : j * total + at + 1] = total_of(hx * f)

    place = lax.broadcasted_iota(jnp.int32, (total, TUBES), 0)
    old = [om[j * total : (j + 1) * total] for j in range(5)]
    half = [hm[j * total : (j + 1) * total] for j in range(5)]
    resid = [half[j] - old[j] for j in range(5)]

    entries = [pb[pl.ds(e, total, stride=PROWS), :] for e in range(75)]

    def apply_block(first, vector):
        out = []
        for i in range(5):
            value = entries[first + i * 5] * vector[0]
            for j in range(1, 5):
                value = value + entries[first + i * 5 + j] * vector[j]
            out.append(value)
        return out

    corr = apply_block(50, resid)
    for _ in range(JACOBI):
        left = [jnp.where(place == 0, 0.0, pltpu.roll(c, 1, 0)) for c in corr]
        right = [jnp.where(place == total - 1, 0.0, pltpu.roll(c, total - 1, 0)) for c in corr]
        lo = apply_block(0, left)
        up = apply_block(25, right)
        corr = apply_block(50, [resid[j] - lo[j] - up[j] for j in range(5)])
    goal = []
    for j in range(5):
        macro = half[j] + corr[j]
        co[j * total : (j + 1) * total] = corr[j]
        mac[j * total : (j + 1) * total] = macro
        if j < 2:
            change = jnp.sum(old[j] - macro, axis=0, keepdims=True)
            goal.append(jnp.sum(change, axis=1, keepdims=True))
    for p in range(length):
        at = s * length + p
        c = [co[pl.ds(j * total + at, 1), :] for j in range(5)]
        for j in range(5):
            macro_out[j : j + 1, p * TUBES : (p + 1) * TUBES] = mac[pl.ds(j * total + at, 1), :]
        t_loc[p * 4 + 0] = t_all[0 * total + at] + (c[0] + x2 * c[1] + en * c[4])
        t_loc[p * 4 + 1] = t_all[1 * total + at] + 2.0 * c[2]
        t_loc[p * 4 + 2] = t_all[2 * total + at] + 2.0 * c[3]
        t_loc[p * 4 + 3] = t_all[3 * total + at] + c[4] * (1.0 / 1.5)

    if square:
        last_waits(0)
        last_waits(1)
    else:

        @pl.when(jnp.logical_not(inner))
        def _():
            for c in range(CHUNKS):
                relay(c)

    def second_pass(k, acc):
        n_mix, p_mix = in_n[k, 16:24], in_p[k, 16:24]
        flow = (
            jnp.concatenate(
                [in_n[k, 0:8], jnp.where(low, n_mix, pltpu.roll(p_mix, 4, 0)), in_p[k, 0:8]], axis=0
            ),
            jnp.concatenate(
                [in_n[k, 8:16], jnp.where(low, pltpu.roll(n_mix, 4, 0), p_mix), in_p[k, 8:16]], axis=0
            ),
        )
        for half_row in range(2):
            at = v * rows + 2 * k + half_row
            here = pl.ds(pl.multiple_of(k * 48, 8) + half_row * 24, 24)
            g = table[at]
            y = table[4 * all_rows + at]
            z = table[5 * all_rows + at]
            e = table[6 * all_rows + at]
            d = [dv[here, p * TUBES : (p + 1) * TUBES] for p in range(length)]
            size = None
            for p in range(length):
                f = t_loc[p * 4] + y * t_loc[p * 4 + 1] + z * t_loc[p * 4 + 2] + e * t_loc[p * 4 + 3]
                f = f + w_tab[p * (length + 1) + length] * flow[half_row]
                for q in range(length):
                    f = f + w_tab[p * (length + 1) + q] * d[q]
                syn[here, p * TUBES : (p + 1) * TUBES] = f
                size = jnp.abs(f) if size is None else size + jnp.abs(f)
            acc = acc + g * size
        return acc

    acc = zero
    stores = []
    for c in range(CHUNKS):
        acc = lax.fori_loop(c * per, (c + 1) * per, second_pass, acc)
        part = pl.ds(c * per * 48, per * 48)
        store = pltpu.make_async_copy(syn.at[part], syn_out.at[part], syn_sem.at[c])
        store.start()
        stores.append(store)

    lane = lax.broadcasted_iota(jnp.int32, (8, TUBES), 1)
    one = jnp.sum(acc, axis=1, keepdims=True)
    packed = jnp.where(lane == 0, one[0:8], jnp.where(lane == 1, one[8:16], one[16:24]))
    ld_own[...] = packed
    b1 = [
        remote(ld_own, ld_rv.at[d - 1], b1_send.at[d - 1], b1_recv.at[d - 1],
               {"vel": lax.rem(v + d, n_vel)})
        for d in range(1, n_vel)
    ]
    for copy in b1:
        copy.start()
    for d in range(1, n_vel):
        b1[d - 1].wait_recv()
        packed = packed + ld_rv[d - 1]
    ld_sec[...] = packed
    b2 = [
        remote(ld_sec, ld_rs.at[d - 1], b2_send.at[d - 1], b2_recv.at[d - 1],
               {"sec": lax.rem(s + d, n_sec)})
        for d in range(1, n_sec)
    ]
    for copy in b2:
        copy.start()
    for d in range(1, n_sec):
        b2[d - 1].wait_recv()
        packed = packed + ld_rs[d - 1]

    signed = cols[24:32, :]
    loaded = cols[32:40, :] * packed

    def everything(value):
        return jnp.sum(jnp.sum(value, axis=0, keepdims=True), axis=1, keepdims=True)

    shift_mass = jnp.zeros((1, 1), jnp.float32)
    shift_flow = jnp.zeros((1, 1), jnp.float32)
    for turn in range(NEWTON):
        if turn == 0:
            scaled = loaded
            miss_mass, miss_flow = -goal[0], -goal[1]
        else:
            growth = jnp.exp(shift_mass + shift_flow * signed)
            scaled = loaded * growth
            excess = loaded * (growth - 1.0)
            miss_mass = everything(excess) - goal[0]
            miss_flow = everything(excess * signed) - goal[1]
        m0 = everything(scaled)
        m1 = everything(scaled * signed)
        m2 = everything(scaled * signed * signed)
        determinant = m0 * m2 - m1 * m1
        new_mass = shift_mass - (m2 * miss_mass - m1 * miss_flow) / determinant
        shift_flow = shift_flow - (m0 * miss_flow - m1 * miss_mass) / determinant
        shift_mass = new_mass
    grow_out[...] = jnp.exp(shift_mass + shift_flow * column(6)) - 1.0

    if square:
        for way in range(2):
            when_role(way, 1, lambda: thr_to(way, 0).wait_send())
            when_role(way, 2, lambda: thr_to(way, 3).wait_send())
    for c in range(CHUNKS):
        stores[c].wait()
        if square:
            sent(0, c)
            sent(1, c)
            continue

        @pl.when(s < n_sec - 1)
        def _():
            pos_copy(c).wait_send()

        @pl.when(s > 0)
        def _():
            neg_copy(c).wait_send()

    for d in range(1, n_vel):
        when_owner(lax.rem(v + d, n_vel), lambda: a1(d).wait_send())
        when_owner(v, lambda: a3(d, mine, lax.rem(v + d, n_vel)).wait_send())
        b1[d - 1].wait_send()
    for d in range(1, n_sec):
        pb_copy(d).wait_send()
        pb_cross(d).wait_send()
        when_owner(v, lambda: a2(d, s, lax.rem(s + d, n_sec)).wait_send())
        b2[d - 1].wait_send()


def body(n_sec, n_vel, distribution, collision, lower_blocks, upper_blocks, diag_inverse):
    nodes, cells = distribution.shape
    length = cells // TUBES
    rows = nodes // NXI
    pairs = rows // 2
    slices = 4 * length
    total = n_sec * length
    row_table, col_table = tables()
    f32 = jnp.float32
    vmem = pl.BlockSpec(memory_space=pltpu.VMEM)
    dma = pltpu.SemaphoreType.DMA
    syn, grow, macro = pl.pallas_call(
        functools.partial(kernel, n_sec, n_vel, length, rows),
        out_shape=(
            jax.ShapeDtypeStruct((nodes, cells), f32),
            jax.ShapeDtypeStruct((NXI, TUBES), f32),
            jax.ShapeDtypeStruct((5, cells), f32),
        ),
        in_specs=[pl.BlockSpec(memory_space=pl.ANY)] * 7,
        out_specs=(pl.BlockSpec(memory_space=pl.ANY), vmem, vmem),
        scratch_shapes=[
            pltpu.SMEM(row_table.shape, f32),
            pltpu.VMEM(col_table.shape, f32),
            pltpu.VMEM((1, cells), f32),
            pltpu.VMEM((25, cells), f32),
            pltpu.VMEM((25, cells), f32),
            pltpu.VMEM((25, cells), f32),
            dma((6,)),
            pltpu.VMEM((nodes, cells), f32),
            pltpu.VMEM((nodes, cells), f32),
            pltpu.VMEM((pairs, 24, TUBES), f32),
            pltpu.VMEM((pairs, 24, TUBES), f32),
            pltpu.VMEM((pairs, 24, TUBES), f32),
            pltpu.VMEM((pairs, 24, TUBES), f32),
            pltpu.VMEM((slices, NXI, TUBES), f32),
            pltpu.VMEM((n_vel - 1, NXI, TUBES), f32),
            pltpu.VMEM((slices, n_sec, NXI, TUBES), f32),
            pltpu.VMEM((total * PROWS, TUBES), f32),
            pltpu.VMEM((5 * total, TUBES), f32),
            pltpu.VMEM((5 * total, TUBES), f32),
            pltpu.VMEM((5 * total, TUBES), f32),
            pltpu.VMEM((5 * total, TUBES), f32),
            pltpu.VMEM((4 * total, NXI, TUBES), f32),
            pltpu.VMEM((length * (length + 1), NXI, TUBES), f32),
            pltpu.VMEM((slices, NXI, TUBES), f32),
            pltpu.VMEM((8, TUBES), f32),
            pltpu.VMEM((8, TUBES), f32),
            pltpu.VMEM((n_vel - 1, 8, TUBES), f32),
            pltpu.VMEM((n_sec - 1, 8, TUBES), f32),
            dma,
            dma((CHUNKS,)), dma((CHUNKS,)), dma((CHUNKS,)), dma((CHUNKS,)), dma((CHUNKS,)),
            dma((n_vel - 1,)), dma((n_vel - 1,)),
            dma((n_sec - 1,)), dma((n_sec - 1,)),
            dma((n_vel - 1,)), dma((n_vel - 1,)),
            dma((n_sec - 1,)), dma((n_sec - 1,)),
            dma((n_vel - 1,)), dma((n_vel - 1,)),
            dma((n_sec - 1,)), dma((n_sec - 1,)),
            pltpu.VMEM((2, pairs, 24, TUBES), f32),
            pltpu.VMEM((2, pairs, 24, TUBES), f32),
            pltpu.VMEM((2, 24, TUBES), f32),
            pltpu.VMEM((2, 24, TUBES), f32),
            dma((2, CHUNKS)), dma((2, CHUNKS)), dma((2, CHUNKS)), dma((2,)), dma((2,)),
            dma((n_sec - 1,)), dma((n_sec - 1,)),
        ],
        compiler_params=pltpu.CompilerParams(
            collective_id=0, has_side_effects=True, vmem_limit_bytes=56 * 1024 * 1024
        ),
    )(
        jnp.asarray(row_table), jnp.asarray(col_table), distribution,
        collision.reshape(1, cells), lower_blocks, upper_blocks, diag_inverse,
    )
    field = syn.reshape(rows, NXI, cells)
    new = field + jnp.abs(field) * grow[None, :, 0:1]
    return (new.reshape(nodes, cells), macro)


def solution(mesh):
    in_specs = (P("vel", "sec"), P("sec"), P(None, "sec"), P(None, "sec"), P(None, "sec"))
    out_specs = (P("vel", "sec"), P(None, "sec"))
    run = functools.partial(body, mesh.shape["sec"], mesh.shape["vel"])
    return jax.shard_map(run, mesh=mesh, in_specs=in_specs, out_specs=out_specs, check_vma=False)
```

```python
import functools
import math

import jax
import jax.numpy as jnp
import numpy as np
from jax import lax
from jax.experimental import pallas as pl
from jax.experimental.pallas import tpu as pltpu
from jax.sharding import PartitionSpec as P

NXI = 24
TUBES = 128
JACOBI = 4
NEWTON = 2
PROWS = 80
pseudo_rate = 1.0
MESH = pl.DeviceIdType.MESH


def hermite_rule(count):
    quarter = math.pi ** (-0.25)
    found = []
    last_slope = 1.0
    for index in range(count // 2):
        if index == 0:
            guess = math.sqrt(2.0 * count + 1.0) - 1.85575 * (2.0 * count + 1.0) ** (-0.16667)
        elif index == 1:
            guess = guess - 1.14 * count**0.426 / guess
        elif index == 2:
            guess = 1.86 * guess - 0.86 * found[0][0]
        elif index == 3:
            guess = 1.91 * guess - 0.91 * found[1][0]
        else:
            guess = 2.0 * guess - found[index - 2][0]
        for repeat in range(60):
            current = quarter
            previous = 0.0
            for order in range(count):
                older = previous
                previous = current
                current = (
                    guess * math.sqrt(2.0 / (order + 1)) * previous
                    - math.sqrt(order / (order + 1.0)) * older
                )
            last_slope = math.sqrt(2.0 * count) * previous
            guess = guess - current / last_slope
        found.append((guess, 2.0 / (last_slope * last_slope)))
    positive = found[::-1]
    points = [-pair[0] for pair in found] + [pair[0] for pair in positive]
    weights = [pair[1] for pair in found] + [pair[1] for pair in positive]
    return (np.array(points), np.array(weights))


def tables():
    points, weights = hermite_rule(NXI)
    h = weights / math.sqrt(math.pi)
    y = np.repeat(points, NXI)
    z = np.tile(points, NXI)
    g = np.repeat(h, NXI) * np.tile(h, NXI)
    e = y * y + z * z - 1.0
    rows = np.concatenate([g, g * y, g * z, g * e, y, z, e]).astype(np.float32)
    cols = np.zeros((40, 128))
    x = points
    listed = [np.abs(x), 2.0 * x, (x * x - 0.5) / 1.5, h, h * x, h * (x * x - 0.5), x]
    for k, column in enumerate(listed):
        cols[:24, k] = column
    for lane in range(3):
        cols[24:32, lane] = x[lane * 8 : lane * 8 + 8]
        cols[32:40, lane] = h[lane * 8 : lane * 8 + 8]
    return rows, cols.astype(np.float32)


def chunks_of(pairs):
    return 12 if pairs % 12 == 0 else 6


def kernel(
    n_sec, n_vel, length, rows,
    table_in, cols_in, dist, coll_in, lower_in, upper_in, diag_in,
    syn_out, grow_out, macro_out,
    table, cols, coll, lower, upper, diag, small_sem,
    dv, syn, out_p, out_n, in_p, in_n, s_part, s_recv, s_all, pb,
    om, hm, co, mac, t_all, w_tab, t_loc, ld_own, ld_sec, ld_rv, ld_rs,
    dist_sem, syn_sem, p_send, p_recv, n_send, n_recv,
    a1_send, a1_recv, a2_send, a2_recv, a3_send, a3_recv,
    pb_send, pb_recv, b1_send, b1_recv, b2_send, b2_recv,
    tmp_a, tmp_b, thr_own, thr_side, y_send, ta_recv, tb_recv, th_send, th_recv, px_send, px_recv,
):
    s = lax.axis_index("sec")
    v = lax.axis_index("vel")
    total = n_sec * length
    slices = 4 * length
    pairs = rows // 2
    chunks = chunks_of(pairs)
    per = pairs // chunks
    all_rows = NXI * NXI

    load = pltpu.make_async_copy(dist, dv, dist_sem)
    small = [
        pltpu.make_async_copy(src, dst, small_sem.at[k])
        for k, (src, dst) in enumerate(
            (
                (cols_in, cols), (coll_in, coll), (table_in, table),
                (lower_in, lower), (upper_in, upper), (diag_in, diag),
            )
        )
    ]
    for copy in small[:3]:
        copy.start()
    load.start()
    for copy in small[3:]:
        copy.start()
    barrier = pltpu.get_barrier_semaphore()
    for d in range(1, n_vel):
        pl.semaphore_signal(
            barrier, inc=1, device_id={"vel": lax.rem(v + d, n_vel)}, device_id_type=MESH
        )
    for d in range(1, n_sec):
        pl.semaphore_signal(
            barrier, inc=1, device_id={"sec": lax.rem(s + d, n_sec)}, device_id_type=MESH
        )

    def remote(src, dst, send, recv, where):
        return pltpu.make_async_remote_copy(
            src_ref=src, dst_ref=dst, send_sem=send, recv_sem=recv,
            device_id=where, device_id_type=MESH,
        )

    def column(k):
        return jnp.broadcast_to(cols[0:24, k : k + 1], (24, TUBES))

    small[0].wait()
    small[1].wait()
    sub = lax.broadcasted_iota(jnp.int32, (8, TUBES), 0)
    low = sub < 4
    pos = lax.broadcasted_iota(jnp.int32, (24, TUBES), 0) >= 12
    reach = column(0) * float(total)

    inv, rate = [], []
    for p in range(length):
        den = reach + coll[0:1, p * TUBES : (p + 1) * TUBES] + pseudo_rate
        i = 1.0 / den
        inv.append(i)
        rate.append(reach * i)
    zero = jnp.zeros((24, TUBES), jnp.float32)
    w = [[zero] * length for _ in range(length)]
    a = [zero] * length
    fw = None
    for p in range(length):
        row = [rate[p] * e for e in fw[0]] + [inv[p]] if fw else [inv[p]]
        carry = rate[p] * fw[1] if fw else rate[p]
        fw = (row, carry)
        for q in range(p + 1):
            w[p][q] = jnp.where(pos, row[q], w[p][q])
        a[p] = jnp.where(pos, carry, a[p])
    bw = None
    for p in reversed(range(length)):
        row = [inv[p]] + [rate[p] * e for e in bw[0]] if bw else [inv[p]]
        carry = rate[p] * bw[1] if bw else rate[p]
        bw = (row, carry)
        for k in range(len(row)):
            w[p][p + k] = jnp.where(pos, w[p][p + k], row[k])
        a[p] = jnp.where(pos, a[p], carry)
    for p in range(length):
        for q in range(length):
            w_tab[p * (length + 1) + q] = w[p][q]
        w_tab[p * (length + 1) + length] = a[p]
    last = [jnp.where(pos, w[length - 1][q], w[0][q]) for q in range(length)]
    through = jnp.where(pos, a[length - 1], a[0])
    mix = through[8:16]
    mix_r = pltpu.roll(mix, 4, 0)
    thr_n = jnp.concatenate([through[0:8], through[0:8], jnp.where(low, mix, mix_r)], axis=0)
    thr_p = jnp.concatenate([through[16:24], through[16:24], jnp.where(low, mix_r, mix)], axis=0)

    @pl.when(s == 0)
    def _():
        in_p[...] = jnp.zeros_like(in_p)

    @pl.when(s == n_sec - 1)
    def _():
        in_n[...] = jnp.zeros_like(in_n)

    pl.semaphore_wait(barrier, n_vel + n_sec - 2)
    small[2].wait()
    load.wait()

    def chunk(c):
        return pl.ds(c * per, per)

    def pos_copy(c):
        to = jnp.minimum(s + 1, n_sec - 1)
        return remote(out_p.at[chunk(c)], in_p.at[chunk(c)], p_send.at[c], p_recv.at[c], {"sec": to})

    def neg_copy(c):
        to = jnp.maximum(s - 1, 0)
        return remote(out_n.at[chunk(c)], in_n.at[chunk(c)], n_send.at[c], n_recv.at[c], {"sec": to})

    square = n_sec == 4
    outs, ins, thrs = (out_p, out_n), (in_p, in_n), (thr_p, thr_n)
    x_sends, in_recvs = (p_send, n_send), (p_recv, n_recv)

    def device_of(way, role):
        return role if way == 0 else 3 - role

    def when_role(way, role, run):
        pl.when(s == device_of(way, role))(run)

    def out_to(way, c, role):
        return remote(outs[way].at[chunk(c)], ins[way].at[chunk(c)], x_sends[way].at[c],
                      in_recvs[way].at[c], {"sec": device_of(way, role)})

    def out_to_a(way, c, role):
        return remote(outs[way].at[chunk(c)], tmp_a.at[way, chunk(c)], x_sends[way].at[c],
                      ta_recv.at[way, c], {"sec": device_of(way, role)})

    def out_to_b(way, c, role):
        return remote(outs[way].at[chunk(c)], tmp_b.at[way, chunk(c)], x_sends[way].at[c],
                      tb_recv.at[way, c], {"sec": device_of(way, role)})

    def a_to(way, c, role):
        return remote(tmp_a.at[way, chunk(c)], ins[way].at[chunk(c)], y_send.at[way, c],
                      in_recvs[way].at[c], {"sec": device_of(way, role)})

    def b_to(way, c, role):
        return remote(tmp_b.at[way, chunk(c)], ins[way].at[chunk(c)], x_sends[way].at[c],
                      in_recvs[way].at[c], {"sec": device_of(way, role)})

    def thr_to(way, role):
        return remote(thr_own.at[way], thr_side.at[way], th_send.at[way],
                      th_recv.at[way], {"sec": device_of(way, role)})

    if square:
        for way in range(2):
            thr_own[way] = thrs[way]
            when_role(way, 1, lambda: thr_to(way, 0).start())
            when_role(way, 2, lambda: thr_to(way, 3).start())

    def launch(way, c):
        if c % 2 == 0:
            when_role(way, 1, lambda: out_to_a(way, c, 0).start())
        else:
            when_role(way, 0, lambda: out_to(way, c, 1).start())
            when_role(way, 2, lambda: out_to_a(way, c, 3).start())

    def near_job(way, i):
        even, odd = 2 * i, 2 * i + 1

        def role_0():
            if i == 0:
                thr_to(way, 1).wait_recv()
            out_to_a(way, even, 1).wait_recv()
            tmp_a[way, chunk(even)] = (
                thr_side[way][None] * outs[way][chunk(even)] + tmp_a[way, chunk(even)]
            )
            a_to(way, even, 2).start()

        def role_1():
            out_to(way, odd, 0).wait_recv()
            outs[way][chunk(odd)] = outs[way][chunk(odd)] + thrs[way][None] * ins[way][chunk(odd)]
            out_to_b(way, odd, 3).start()

        when_role(way, 0, role_0)
        when_role(way, 1, role_1)

    def far_job(way, i):
        even, odd = 2 * i, 2 * i + 1

        def role_2():
            out_to(way, even, 3).wait_recv()
            outs[way][chunk(even)] = outs[way][chunk(even)] + thrs[way][None] * ins[way][chunk(even)]
            out_to(way, even, 3).start()

        def role_3():
            if i == 0:
                thr_to(way, 2).wait_recv()
            out_to_b(way, odd, 1).wait_recv()
            b_to(way, odd, 2).start()
            out_to_a(way, odd, 2).wait_recv()
            ins[way][chunk(odd)] = (
                thr_side[way][None] * tmp_b[way, chunk(odd)] + tmp_a[way, chunk(odd)]
            )

        when_role(way, 2, role_2)
        when_role(way, 3, role_3)

    def last_wait(way, c):
        if c % 2 == 0:
            when_role(way, 1, lambda: out_to(way, c, 2).wait_recv())
            when_role(way, 3, lambda: out_to(way, c, 2).wait_recv())
        else:
            when_role(way, 2, lambda: out_to(way, c, 3).wait_recv())

    def sent(way, c):
        when_role(way, 0, lambda: out_to(way, c, 1).wait_send())
        if c % 2 == 0:
            when_role(way, 0, lambda: a_to(way, c, 2).wait_send())
            when_role(way, 1, lambda: out_to_a(way, c, 0).wait_send())
            when_role(way, 2, lambda: out_to(way, c, 3).wait_send())
        else:
            when_role(way, 1, lambda: out_to_b(way, c, 3).wait_send())
            when_role(way, 2, lambda: out_to_a(way, c, 3).wait_send())
            when_role(way, 3, lambda: b_to(way, c, 2).wait_send())

    def first_pass(k, acc):
        acc = list(acc)
        bs = []
        for half in range(2):
            r = 2 * k + half
            at = v * rows + r
            d = [
                dv[pl.ds(pl.multiple_of(k * 48, 8) + half * 24, 24), p * TUBES : (p + 1) * TUBES]
                for p in range(length)
            ]
            for q in range(4):
                scale = table[q * all_rows + at]
                for p in range(length):
                    acc[p * 4 + q] = acc[p * 4 + q] + scale * d[p]
            b = last[0] * d[0]
            for p in range(1, length):
                b = b + last[p] * d[p]
            bs.append(b)
        b0, b1 = bs
        out_n[k, 0:8] = b0[0:8]
        out_n[k, 8:16] = b1[0:8]
        out_n[k, 16:24] = jnp.where(low, b0[8:16], pltpu.roll(b1[8:16], 4, 0))
        out_p[k, 0:8] = b0[16:24]
        out_p[k, 8:16] = b1[16:24]
        out_p[k, 16:24] = jnp.where(low, pltpu.roll(b0[8:16], 4, 0), b1[8:16])
        return tuple(acc)

    acc = (zero,) * slices
    for c in range(chunks):
        acc = lax.fori_loop(c * per, (c + 1) * per, first_pass, acc)
        if square:
            launch(0, c)
            launch(1, c)
            continue

        @pl.when(s == 0)
        def _():
            pos_copy(c).start()

        @pl.when(s == n_sec - 1)
        def _():
            neg_copy(c).start()

    for k in range(slices):
        s_part[k] = acc[k]

    def when_owner(index, run):
        if n_vel == slices:
            run()
        else:
            pl.when(index < slices)(run)

    def a1(d):
        to = lax.rem(v + d, n_vel)
        slot = jnp.minimum(to, slices - 1)
        return remote(s_part.at[slot], s_recv.at[d - 1], a1_send.at[d - 1], a1_recv.at[d - 1], {"vel": to})

    for d in range(1, n_vel):
        when_owner(lax.rem(v + d, n_vel), lambda: a1(d).start())

    for copy in small[3:]:
        copy.wait()
    for p in range(length):
        lanes = slice(p * TUBES, (p + 1) * TUBES)
        base = (s * length + p) * PROWS
        for k, block in enumerate((lower, upper, diag)):
            for e in range(25):
                pb[pl.ds(base + k * 25 + e, 1), :] = block[e : e + 1, lanes]
        pb[pl.ds(base + 75, 1), :] = coll[0:1, lanes]
    core = lax.rem(v, 2)
    share = length * PROWS // 2

    def half_of(sec, which):
        return pl.ds((sec * 2 + which) * share, share)

    def pb_copy(d):
        to = lax.rem(s + d, n_sec)
        mine_rows = pb.at[half_of(s, core)]
        return remote(mine_rows, mine_rows, pb_send.at[d - 1], pb_recv.at[d - 1], {"sec": to})

    def pb_wait(d):
        frm = lax.rem(s + n_sec - d, n_sec)
        there = pb.at[half_of(frm, core)]
        remote(there, there, pb_send.at[d - 1], pb_recv.at[d - 1], {"sec": frm}).wait_recv()

    def pb_cross(d, other=0):
        frm = lax.rem(s + n_sec - d, n_sec)
        there = pb.at[half_of(frm, core + other * (1 - 2 * core))]
        return remote(there, there, px_send.at[d - 1], px_recv.at[d - 1], {"vel": v + 1 - 2 * core})


    mine = jnp.minimum(v, slices - 1)

    def a2(d, slot, to):
        return remote(
            s_all.at[mine, slot], s_all.at[mine, slot], a2_send.at[d - 1], a2_recv.at[d - 1], {"sec": to}
        )

    def reduce_slices():
        got = s_part[mine]
        for d in range(1, n_vel):
            a1(d).wait_recv()
            got = got + s_recv[d - 1]
        s_all[mine, s] = got
        for d in range(1, n_sec):
            a2(d, s, lax.rem(s + d, n_sec)).start()


    when_owner(v, reduce_slices)
    if square:
        for c in range(0, chunks, 2):
            when_role(0, 0, lambda: out_to(0, c, 1).start())
            when_role(1, 0, lambda: out_to(1, c, 1).start())
    for d in range(1, n_sec):
        pb_copy(d).start()

    def relay(c):
        def forward_pos():
            pos_copy(c).wait_recv()

            @pl.when(s < n_sec - 1)
            def _():
                out_p[chunk(c)] = out_p[chunk(c)] + thr_p[None] * in_p[chunk(c)]
                pos_copy(c).start()

        def forward_neg():
            neg_copy(c).wait_recv()

            @pl.when(s > 0)
            def _():
                out_n[chunk(c)] = out_n[chunk(c)] + thr_n[None] * in_n[chunk(c)]
                neg_copy(c).start()

        @pl.when(s < n_sec // 2)
        def _():
            pl.when(s > 0)(forward_pos)
            forward_neg()

        @pl.when(s >= n_sec // 2)
        def _():
            pl.when(s < n_sec - 1)(forward_neg)
            forward_pos()

    def a3(d, slot, to):
        return remote(s_all.at[slot], s_all.at[slot], a3_send.at[d - 1], a3_recv.at[d - 1], {"vel": to})

    def gather_slices():
        for d in range(1, n_sec):
            frm = lax.rem(s + n_sec - d, n_sec)
            a2(d, frm, frm).wait_recv()
        for d in range(1, n_vel):
            a3(d, mine, lax.rem(v + d, n_vel)).start()

    if square:
        pl.when(s < 2)(lambda: near_job(0, 0))
        pl.when(s >= 2)(lambda: near_job(1, 0))
    when_owner(v, gather_slices)
    inner = jnp.logical_and(s > 0, s < n_sec - 1)

    if square:
        steps = chunks // 2

        def jobs(first, second):
            for i in range(steps + 1):
                if 0 < i < steps:
                    near_job(first, i)
                if i > 0:
                    far_job(second, i - 1)

        pl.when(s < 2)(lambda: jobs(0, 1))
        pl.when(s >= 2)(lambda: jobs(1, 0))
    else:

        @pl.when(inner)
        def _():
            for c in range(chunks):
                relay(c)

    for d in range(1, n_sec):
        pb_wait(d)
        pb_cross(d).start()
    for d in range(1, n_vel):
        frm = lax.rem(v + n_vel - d, n_vel)
        when_owner(frm, lambda: a3(d, jnp.minimum(frm, slices - 1), frm).wait_recv())
    for d in range(1, n_sec):
        pb_cross(d, 1).wait_recv()

    hx, hxx, hxe = column(3), column(4), column(5)
    x2, en = column(1), column(2)

    def total_of(value):
        return jnp.sum(value, axis=0, keepdims=True)

    for at in range(total):
        sec, p = at // length, at % length
        s0, s2, s3, s4 = [s_all[p * 4 + q, sec] for q in range(4)]
        om[0 * total + at : 0 * total + at + 1] = total_of(hx * s0)
        om[1 * total + at : 1 * total + at + 1] = total_of(hxx * s0)
        om[2 * total + at : 2 * total + at + 1] = total_of(hx * s2)
        om[3 * total + at : 3 * total + at + 1] = total_of(hx * s3)
        om[4 * total + at : 4 * total + at + 1] = total_of(hxe * s0 + hx * s4)

    thick, invs, rates = [], [], []
    for at in range(total):
        t = pb[at * PROWS + 75 : at * PROWS + 76]
        i = 1.0 / (reach + t + pseudo_rate)
        thick.append(t)
        invs.append(i)
        rates.append(reach * i)
    turned = [jnp.where(pos, rates[i], rates[total - 1 - i]) for i in range(total)]

    def sweep(drive):
        found, carried = [], None
        for i in range(total):
            here = jnp.where(pos, drive[i], drive[total - 1 - i])
            carried = here if carried is None else turned[i] * carried + here
            found.append(carried)
        return [jnp.where(pos, found[i], found[total - 1 - i]) for i in range(total)]

    halves = {}
    for q, norm in enumerate((1.0, 0.5, 0.5, 1.0)):
        goals, parts = [], []
        for at in range(total):
            m = [om[j * total + at : j * total + at + 1] for j in range(5)]
            if q == 0:
                goal = thick[at] * (m[0] + x2 * m[1] + en * m[4])
            elif q == 3:
                goal = jnp.broadcast_to(thick[at] * m[4] * (1.0 / 1.5), (24, TUBES))
            else:
                goal = jnp.broadcast_to(thick[at] * m[q + 1] * 2.0, (24, TUBES))
            sec, p = at // length, at % length
            goals.append(goal * invs[at])
            parts.append((s_all[p * 4 + q, sec] + norm * goal) * invs[at])
        swept = sweep(goals)
        for at in range(total):
            t_all[q * total + at] = swept[at]
        swept = sweep(parts)
        for at in range(total):
            f = swept[at]
            if q == 0:
                hm[at : at + 1] = total_of(hx * f)
                hm[total + at : total + at + 1] = total_of(hxx * f)
                halves[at] = hxe * f
            elif q == 3:
                hm[4 * total + at : 4 * total + at + 1] = total_of(halves[at] + hx * f)
            else:
                j = q + 1
                hm[j * total + at : j * total + at + 1] = total_of(hx * f)

    place = lax.broadcasted_iota(jnp.int32, (total, TUBES), 0)
    old = [om[j * total : (j + 1) * total] for j in range(5)]
    half = [hm[j * total : (j + 1) * total] for j in range(5)]
    resid = [half[j] - old[j] for j in range(5)]

    entries = [pb[pl.ds(e, total, stride=PROWS), :] for e in range(75)]

    def apply_block(first, vector):
        out = []
        for i in range(5):
            value = entries[first + i * 5] * vector[0]
            for j in range(1, 5):
                value = value + entries[first + i * 5 + j] * vector[j]
            out.append(value)
        return out

    corr = apply_block(50, resid)
    for _ in range(JACOBI):
        left = [jnp.where(place == 0, 0.0, pltpu.roll(c, 1, 0)) for c in corr]
        right = [jnp.where(place == total - 1, 0.0, pltpu.roll(c, total - 1, 0)) for c in corr]
        lo = apply_block(0, left)
        up = apply_block(25, right)
        corr = apply_block(50, [resid[j] - lo[j] - up[j] for j in range(5)])
    goal = []
    for j in range(5):
        macro = half[j] + corr[j]
        co[j * total : (j + 1) * total] = corr[j]
        mac[j * total : (j + 1) * total] = macro
        if j < 2:
            change = jnp.sum(old[j] - macro, axis=0, keepdims=True)
            goal.append(jnp.sum(change, axis=1, keepdims=True))
    for p in range(length):
        at = s * length + p
        c = [co[pl.ds(j * total + at, 1), :] for j in range(5)]
        for j in range(5):
            macro_out[j : j + 1, p * TUBES : (p + 1) * TUBES] = mac[pl.ds(j * total + at, 1), :]
        t_loc[p * 4 + 0] = t_all[0 * total + at] + (c[0] + x2 * c[1] + en * c[4])
        t_loc[p * 4 + 1] = t_all[1 * total + at] + 2.0 * c[2]
        t_loc[p * 4 + 2] = t_all[2 * total + at] + 2.0 * c[3]
        t_loc[p * 4 + 3] = t_all[3 * total + at] + c[4] * (1.0 / 1.5)

    if not square:

        @pl.when(jnp.logical_not(inner))
        def _():
            for c in range(chunks):
                relay(c)

    def second_pass(k, acc):
        n_mix, p_mix = in_n[k, 16:24], in_p[k, 16:24]
        flow = (
            jnp.concatenate(
                [in_n[k, 0:8], jnp.where(low, n_mix, pltpu.roll(p_mix, 4, 0)), in_p[k, 0:8]], axis=0
            ),
            jnp.concatenate(
                [in_n[k, 8:16], jnp.where(low, pltpu.roll(n_mix, 4, 0), p_mix), in_p[k, 8:16]], axis=0
            ),
        )
        for half_row in range(2):
            at = v * rows + 2 * k + half_row
            here = pl.ds(pl.multiple_of(k * 48, 8) + half_row * 24, 24)
            g = table[at]
            y = table[4 * all_rows + at]
            z = table[5 * all_rows + at]
            e = table[6 * all_rows + at]
            d = [dv[here, p * TUBES : (p + 1) * TUBES] for p in range(length)]
            size = None
            for p in range(length):
                f = t_loc[p * 4] + y * t_loc[p * 4 + 1] + z * t_loc[p * 4 + 2] + e * t_loc[p * 4 + 3]
                f = f + w_tab[p * (length + 1) + length] * flow[half_row]
                for q in range(length):
                    f = f + w_tab[p * (length + 1) + q] * d[q]
                syn[here, p * TUBES : (p + 1) * TUBES] = f
                size = jnp.abs(f) if size is None else size + jnp.abs(f)
            acc = acc + g * size
        return acc

    acc = zero
    stores = []
    for c in range(chunks):
        if square:
            last_wait(0, c)
            last_wait(1, c)
        acc = lax.fori_loop(c * per, (c + 1) * per, second_pass, acc)
        part = pl.ds(c * per * 48, per * 48)
        store = pltpu.make_async_copy(syn.at[part], syn_out.at[part], syn_sem.at[c])
        store.start()
        stores.append(store)

    lane = lax.broadcasted_iota(jnp.int32, (8, TUBES), 1)
    one = jnp.sum(acc, axis=1, keepdims=True)
    packed = jnp.where(lane == 0, one[0:8], jnp.where(lane == 1, one[8:16], one[16:24]))
    ld_own[...] = packed
    b1 = [
        remote(ld_own, ld_rv.at[d - 1], b1_send.at[d - 1], b1_recv.at[d - 1],
               {"vel": lax.rem(v + d, n_vel)})
        for d in range(1, n_vel)
    ]
    for copy in b1:
        copy.start()
    for d in range(1, n_vel):
        b1[d - 1].wait_recv()
        packed = packed + ld_rv[d - 1]
    ld_sec[...] = packed
    b2 = [
        remote(ld_sec, ld_rs.at[d - 1], b2_send.at[d - 1], b2_recv.at[d - 1],
               {"sec": lax.rem(s + d, n_sec)})
        for d in range(1, n_sec)
    ]
    for copy in b2:
        copy.start()
    for d in range(1, n_sec):
        b2[d - 1].wait_recv()
        packed = packed + ld_rs[d - 1]

    signed = cols[24:32, :]
    loaded = cols[32:40, :] * packed

    def everything(value):
        return jnp.sum(jnp.sum(value, axis=0, keepdims=True), axis=1, keepdims=True)

    shift_mass = jnp.zeros((1, 1), jnp.float32)
    shift_flow = jnp.zeros((1, 1), jnp.float32)
    for turn in range(NEWTON):
        if turn == 0:
            scaled = loaded
            miss_mass, miss_flow = -goal[0], -goal[1]
        else:
            growth = jnp.exp(shift_mass + shift_flow * signed)
            scaled = loaded * growth
            excess = loaded * (growth - 1.0)
            miss_mass = everything(excess) - goal[0]
            miss_flow = everything(excess * signed) - goal[1]
        m0 = everything(scaled)
        m1 = everything(scaled * signed)
        m2 = everything(scaled * signed * signed)
        determinant = m0 * m2 - m1 * m1
        new_mass = shift_mass - (m2 * miss_mass - m1 * miss_flow) / determinant
        shift_flow = shift_flow - (m0 * miss_flow - m1 * miss_mass) / determinant
        shift_mass = new_mass
    grown = jnp.exp(shift_mass + shift_flow * column(6)) - 1.0
    for p in range(length):
        grow_out[:, p * TUBES : (p + 1) * TUBES] = grown

    if square:
        for way in range(2):
            when_role(way, 1, lambda: thr_to(way, 0).wait_send())
            when_role(way, 2, lambda: thr_to(way, 3).wait_send())
    for c in range(chunks):
        stores[c].wait()
        if square:
            sent(0, c)
            sent(1, c)
            continue

        @pl.when(s < n_sec - 1)
        def _():
            pos_copy(c).wait_send()

        @pl.when(s > 0)
        def _():
            neg_copy(c).wait_send()

    for d in range(1, n_vel):
        when_owner(lax.rem(v + d, n_vel), lambda: a1(d).wait_send())
        when_owner(v, lambda: a3(d, mine, lax.rem(v + d, n_vel)).wait_send())
        b1[d - 1].wait_send()
    for d in range(1, n_sec):
        pb_copy(d).wait_send()
        pb_cross(d).wait_send()
        when_owner(v, lambda: a2(d, s, lax.rem(s + d, n_sec)).wait_send())
        b2[d - 1].wait_send()


def body(n_sec, n_vel, distribution, collision, lower_blocks, upper_blocks, diag_inverse):
    nodes, cells = distribution.shape
    length = cells // TUBES
    rows = nodes // NXI
    pairs = rows // 2
    slices = 4 * length
    chunks = chunks_of(pairs)
    total = n_sec * length
    row_table, col_table = tables()
    f32 = jnp.float32
    vmem = pl.BlockSpec(memory_space=pltpu.VMEM)
    dma = pltpu.SemaphoreType.DMA
    syn, grow, macro = pl.pallas_call(
        functools.partial(kernel, n_sec, n_vel, length, rows),
        out_shape=(
            jax.ShapeDtypeStruct((nodes, cells), f32),
            jax.ShapeDtypeStruct((NXI, cells), f32),
            jax.ShapeDtypeStruct((5, cells), f32),
        ),
        in_specs=[pl.BlockSpec(memory_space=pl.ANY)] * 7,
        out_specs=(pl.BlockSpec(memory_space=pl.ANY), vmem, vmem),
        scratch_shapes=[
            pltpu.SMEM(row_table.shape, f32),
            pltpu.VMEM(col_table.shape, f32),
            pltpu.VMEM((1, cells), f32),
            pltpu.VMEM((25, cells), f32),
            pltpu.VMEM((25, cells), f32),
            pltpu.VMEM((25, cells), f32),
            dma((6,)),
            pltpu.VMEM((nodes, cells), f32),
            pltpu.VMEM((nodes, cells), f32),
            pltpu.VMEM((pairs, 24, TUBES), f32),
            pltpu.VMEM((pairs, 24, TUBES), f32),
            pltpu.VMEM((pairs, 24, TUBES), f32),
            pltpu.VMEM((pairs, 24, TUBES), f32),
            pltpu.VMEM((slices, NXI, TUBES), f32),
            pltpu.VMEM((n_vel - 1, NXI, TUBES), f32),
            pltpu.VMEM((slices, n_sec, NXI, TUBES), f32),
            pltpu.VMEM((total * PROWS, TUBES), f32),
            pltpu.VMEM((5 * total, TUBES), f32),
            pltpu.VMEM((5 * total, TUBES), f32),
            pltpu.VMEM((5 * total, TUBES), f32),
            pltpu.VMEM((5 * total, TUBES), f32),
            pltpu.VMEM((4 * total, NXI, TUBES), f32),
            pltpu.VMEM((length * (length + 1), NXI, TUBES), f32),
            pltpu.VMEM((slices, NXI, TUBES), f32),
            pltpu.VMEM((8, TUBES), f32),
            pltpu.VMEM((8, TUBES), f32),
            pltpu.VMEM((n_vel - 1, 8, TUBES), f32),
            pltpu.VMEM((n_sec - 1, 8, TUBES), f32),
            dma,
            dma((chunks,)), dma((chunks,)), dma((chunks,)), dma((chunks,)), dma((chunks,)),
            dma((n_vel - 1,)), dma((n_vel - 1,)),
            dma((n_sec - 1,)), dma((n_sec - 1,)),
            dma((n_vel - 1,)), dma((n_vel - 1,)),
            dma((n_sec - 1,)), dma((n_sec - 1,)),
            dma((n_vel - 1,)), dma((n_vel - 1,)),
            dma((n_sec - 1,)), dma((n_sec - 1,)),
            pltpu.VMEM((2, pairs, 24, TUBES), f32),
            pltpu.VMEM((2, pairs, 24, TUBES), f32),
            pltpu.VMEM((2, 24, TUBES), f32),
            pltpu.VMEM((2, 24, TUBES), f32),
            dma((2, chunks)), dma((2, chunks)), dma((2, chunks)), dma((2,)), dma((2,)),
            dma((n_sec - 1,)), dma((n_sec - 1,)),
        ],
        compiler_params=pltpu.CompilerParams(
            collective_id=0, has_side_effects=True, vmem_limit_bytes=56 * 1024 * 1024
        ),
    )(
        jnp.asarray(row_table), jnp.asarray(col_table), distribution,
        collision.reshape(1, cells), lower_blocks, upper_blocks, diag_inverse,
    )
    field = syn.reshape(rows, NXI, cells)
    new = field + jnp.abs(field) * grow[None]
    return (new.reshape(nodes, cells), macro)


def solution(mesh):
    in_specs = (P("vel", "sec"), P("sec"), P(None, "sec"), P(None, "sec"), P(None, "sec"))
    out_specs = (P("vel", "sec"), P(None, "sec"))
    run = functools.partial(body, mesh.shape["sec"], mesh.shape["vel"])
    return jax.shard_map(run, mesh=mesh, in_specs=in_specs, out_specs=out_specs, check_vma=False)
```
